256 devices in a mesh: layer: 32 (over y, z), seq: 8 (over x, core).
Axes of the slice: x: 4, y: 4, z: 8, core: 2. Of those that a mesh axis runs over, the one named last changes fastest.
Arguments:
- states: bfloat16 [32, 1024, 1024], P('layer', 'seq'), may hold values from -8 to 8
- w_qkv: bfloat16 [32, 3, 1024, 512], P('layer'), may hold values from -0.1875 to 0.1875
- w_out: bfloat16 [32, 512, 1024], P('layer'), may hold values from -0.25 to 0.25
- norm_gain: float32 [32, 1024], P('layer'), may hold values from 0.25 to 1.75
- qk_gain: float32 [32, 2, 64], P('layer'), may hold values from 0.25 to 1.75
Outputs:
- corrected: bfloat16 [32, 1024, 1024], P('layer', 'seq')
The draws below stay inside these ranges and needn't reach their ends.
All inputs are finite; a program needn't handle non-finite values.
Results may differ from the reference program's by a relative error of at most 0.034.
Values may be sent and summed in bfloat16 or wider, within the bound.
A program may use at most 64 MiB of HBM per device.

```python
import jax
import jax.numpy as jnp
from jax import lax

D = 1024
HEADS = 8
HEAD = 64
TOKENS = 1024
LAYERS = 32


def draw_states(key, part):
    key = jax.random.fold_in(key, 11)
    noise_key = jax.random.fold_in(key, 0)
    noise = jax.random.normal(noise_key, (LAYERS, TOKENS, D), jnp.float32)
    values = noise
    return jnp.clip(values, -8.0, 8.0).astype(jnp.bfloat16)


def level_of(stream_key, dims, cuts, low, top_value):
    def one(position, shards_of):
        draws = jax.random.uniform(jax.random.fold_in(jax.random.fold_in(stream_key, 6), position), (shards_of,), jnp.float32, low / len(cuts), top_value / len(cuts))
        return jnp.repeat(jnp.exp(draws), dims[position] // shards_of).reshape((-1,) + (1,) * (len(dims) - position - 1))

    factor_of = one(*cuts[0])
    for cut in cuts[1:]:
        factor_of = factor_of * one(*cut)
    return factor_of


def bell_draw(rng, dims, deviation, bound, cuts=(), kind=jnp.bfloat16):
    result = jax.random.normal(rng, dims, jnp.float32) * deviation
    if len(cuts) > 0:
        result = level_of(rng, dims, cuts, -0.22, 0.18) * result
    return jnp.clip(result, min=-bound, max=bound).astype(kind)


def setup_inputs(seed: int = 0) -> dict:
    seeds = jax.random.split(jax.random.key(seed), 6)
    states = draw_states(jax.random.fold_in(seeds[5], 71), 0)
    w_qkv = bell_draw(seeds[1], (LAYERS, 3, D, HEADS * HEAD), D ** -0.5, 0.1875, ((0, 32),))
    w_out = bell_draw(seeds[2], (LAYERS, HEADS * HEAD, D), (HEADS * HEAD) ** -0.5, 0.25, ((0, 32),))
    norm_gain = jnp.clip(1.0 + 0.15 * jax.random.normal(seeds[3], (LAYERS, D), jnp.float32), 0.25, 1.75)
    qk_gain = jnp.clip(1.0 + 0.15 * jax.random.normal(seeds[4], (LAYERS, 2, HEAD), jnp.float32), 0.25, 1.75)
    return {"states": states, "w_qkv": w_qkv, "w_out": w_out, "norm_gain": norm_gain, "qk_gain": qk_gain}


epsilon = 1e-06
step_size = 1.0

def normalize(state_rows, gain_vector):
    values_f = state_rows.astype(jnp.float32)
    inverse_rms = lax.rsqrt(lax.optimization_barrier(jnp.mean(values_f * values_f, axis=-1, keepdims=True)) + epsilon)
    return (values_f * inverse_rms * gain_vector.astype(jnp.float32)).astype(jnp.bfloat16)

def head_norm(product, gain_vector):
    head_width = gain_vector.shape[-1]
    split_heads = product.reshape(product.shape[0], -1, head_width)
    inverse_rms = lax.rsqrt(lax.optimization_barrier(jnp.mean(split_heads * split_heads, axis=-1, keepdims=True)) + epsilon)
    return (split_heads * inverse_rms * gain_vector.astype(jnp.float32)).astype(jnp.bfloat16)

def attend(queries, key_rows, value_rows, positions, weight_out):
    head_width = queries.shape[-1]
    scores = jnp.einsum('qhe,khe->hqk', queries.astype(jnp.float32), key_rows.astype(jnp.float32)) * head_width ** (-0.5)
    key_positions = jnp.arange(key_rows.shape[0], dtype=jnp.int32)
    visible = key_positions[None, None, :] <= positions[None, :, None]
    weights = jnp.where(visible, jnp.exp(scores), 0.0)
    probabilities = (weights / lax.optimization_barrier(jnp.sum(weights, axis=-1, keepdims=True))).astype(jnp.bfloat16)
    mixture = jnp.einsum('hqk,khe->qhe', probabilities.astype(jnp.float32), value_rows.astype(jnp.float32)).astype(jnp.bfloat16)
    return jnp.dot(mixture.reshape(queries.shape[0], -1), weight_out, preferred_element_type=jnp.float32)

def reference(states, w_qkv, w_out, norm_gain, qk_gain):
    layer_count = states.shape[0]
    pair_count = layer_count // 2
    positions = jnp.arange(states.shape[1], dtype=jnp.int32)

    def exact(state_rows, layer_index):
        normed = normalize(state_rows, norm_gain[layer_index])
        queries = head_norm(jnp.dot(normed, w_qkv[layer_index, 0], preferred_element_type=jnp.float32), qk_gain[layer_index, 0])
        key_rows = head_norm(jnp.dot(normed, w_qkv[layer_index, 1], preferred_element_type=jnp.float32), qk_gain[layer_index, 1])
        value_rows = jnp.dot(normed, w_qkv[layer_index, 2], preferred_element_type=jnp.float32).astype(jnp.bfloat16)
        value_rows = value_rows.reshape(key_rows.shape)
        return (attend(queries, key_rows, value_rows, positions, w_out[layer_index]), key_rows, value_rows)
    held_keys = []
    guesses = []
    fine_terms = []
    for pair_index in range(pair_count):
        even_layer = 2 * pair_index
        start_state = states[even_layer].astype(jnp.float32)
        branch, key_rows, value_rows = exact(states[even_layer], even_layer)
        fine_state = (start_state + step_size * branch).astype(jnp.bfloat16)
        guesses.append((start_state + 2.0 * step_size * branch).astype(jnp.bfloat16))
        odd_branch, _, _ = exact(fine_state, even_layer + 1)
        fine_terms.append((fine_state.astype(jnp.float32) + step_size * odd_branch).astype(jnp.bfloat16))
        held_keys.append((key_rows, value_rows))
    coarse_state = states[0]
    coarse_states = [coarse_state]
    for pair_index in range(pair_count):
        even_layer = 2 * pair_index
        normed = normalize(coarse_state, norm_gain[even_layer])
        queries = head_norm(jnp.dot(normed, w_qkv[even_layer, 0], preferred_element_type=jnp.float32), qk_gain[even_layer, 0])
        branch = attend(queries, held_keys[pair_index][0], held_keys[pair_index][1], positions, w_out[even_layer])
        correction = fine_terms[pair_index].astype(jnp.float32) - guesses[pair_index].astype(jnp.float32)
        coarse_state = (coarse_state.astype(jnp.float32) + 2.0 * step_size * branch + correction).astype(jnp.bfloat16)
        coarse_states.append(coarse_state)
    corrected = []
    for pair_index in range(pair_count):
        branch, _, _ = exact(coarse_states[pair_index], 2 * pair_index)
        corrected.append((coarse_states[pair_index].astype(jnp.float32) + step_size * branch).astype(jnp.bfloat16))
        corrected.append(coarse_states[pair_index + 1])
    return jnp.stack(corrected)
```

```python
import functools

import jax
import jax.numpy as jnp
from jax import lax
from jax.experimental import pallas as pl
from jax.experimental.pallas import tpu as pltpu
from jax.sharding import PartitionSpec as P

EPS = 1e-06
MESH = pl.DeviceIdType.MESH
F32 = jnp.float32
BF16 = jnp.bfloat16
NT = (((1,), (1,)), ((), ()))
LOG2E = 1.4426950408889634
HEAD = 64
PACK = 4
CHUNK = 16


def dot(a, b):
    return jnp.dot(a, b, preferred_element_type=F32)


def spread_queries(q, mean_square, gain):
    rows, width = q.shape
    heads = width // HEAD
    row_head = lax.broadcasted_iota(jnp.int32, (heads, rows, width), 0)
    col_head = lax.broadcasted_iota(jnp.int32, (heads, rows, width), 2) // HEAD
    spread = jnp.where(row_head == col_head, q[None], 0.0)
    head_square = jnp.sum(spread * spread, axis=-1, keepdims=True) / HEAD
    scale = lax.rsqrt(head_square + EPS * (mean_square[None] + EPS)) * (LOG2E / 8.0)
    packed = (spread * gain).astype(BF16).reshape(heads * rows, width)
    return packed, scale.reshape(heads * rows, 1)


def mix_heads(q, mean_square, gain, kv, first_position):
    rows, width = q.shape
    tokens = kv.shape[0]
    packed, scale = spread_queries(q, mean_square, gain)
    many, wide = PACK * rows, PACK * HEAD
    outs = []
    for g in range(width // wide):
        these = slice(g * many, (g + 1) * many)
        scores = lax.dot_general(
            packed[these, g * wide:(g + 1) * wide], kv[:, g * wide:(g + 1) * wide], NT,
            preferred_element_type=F32,
        ) * scale[these]
        key_at = lax.broadcasted_iota(jnp.int32, (PACK, rows, tokens), 2).reshape(many, tokens)
        query_at = lax.broadcasted_iota(jnp.int32, (PACK, rows, tokens), 1).reshape(many, tokens)
        weights = jnp.where(key_at <= query_at + first_position, jnp.exp2(scores), 0.0)
        total = jnp.sum(weights, axis=-1, keepdims=True)
        mixed = dot(weights.astype(BF16), kv[:, width + g * wide:width + (g + 1) * wide])
        mixed = (mixed * (1.0 / total)).reshape(PACK, rows, wide)
        row_head = lax.broadcasted_iota(jnp.int32, (PACK, rows, wide), 0)
        col_head = lax.broadcasted_iota(jnp.int32, (PACK, rows, wide), 2) // HEAD
        outs.append(jnp.sum(jnp.where(row_head == col_head, mixed, 0.0), axis=0).astype(BF16))
    return jnp.concatenate(outs, axis=-1)


def kernel(layers, seqs, x_ref, wqkv, wo, gain_ref, qk_ref, out_ref,
           kv_held, kv_last, xs, base, fine_out, fine_in, term_in, cin, cout, nxt,
           ga_send, ga_recv, gb_send, gb_recv, fine_sem, term_sem, c_send, c_recv, n_send, n_recv):
    layer = lax.axis_index("layer")
    seq = lax.axis_index("seq")
    rows, width = x_ref.shape
    inner = wo.shape[0]
    chunks = rows // CHUNK
    even = lax.rem(layer, 2) == 0
    odd = jnp.logical_not(even)
    sibling = seq + 1 - 2 * lax.rem(seq, 2)

    barrier = pltpu.get_barrier_semaphore()
    for step in range(1, seqs):
        pl.semaphore_signal(barrier, inc=1, device_id={"seq": lax.rem(seq + step, seqs)}, device_id_type=MESH)
    for step in (-2, -1, 1, 2):
        other = layer + step

        @pl.when(jnp.logical_and(other >= 0, other < layers))
        def _():
            pl.semaphore_signal(barrier, inc=1, device_id={"layer": other}, device_id_type=MESH)

    near = sum(jnp.where(jnp.logical_and(layer + step >= 0, layer + step < layers), 1, 0) for step in (-2, -1, 1, 2))
    pl.semaphore_wait(barrier, seqs - 1 + near)

    def block(ref, index):
        return ref.at[pl.ds(pl.multiple_of(index * rows, rows), rows)]

    def gather_copy(kv, send, recv, slot, index, target):
        return pltpu.make_async_remote_copy(
            src_ref=block(kv, index), dst_ref=block(kv, index), send_sem=send.at[slot], recv_sem=recv.at[index],
            device_id={"seq": target}, device_id_type=MESH)

    def exact(kv, send, recv):
        x = xs[...]
        mean_square = jnp.mean(x * x, axis=-1, keepdims=True)
        y = (x * gain_ref[...]).astype(BF16)
        k = dot(y, wqkv[1])
        same = lax.broadcasted_iota(jnp.int32, (inner, inner), 0) // HEAD
        same = same == lax.broadcasted_iota(jnp.int32, (inner, inner), 1) // HEAD
        head_square = dot((k * k).astype(BF16), same.astype(BF16)) / HEAD
        k = k * lax.rsqrt(head_square + EPS * (mean_square + EPS)) * qk_ref[1:2, :]
        here = pl.ds(pl.multiple_of(seq * rows, rows), rows)
        kv[here, 0:inner] = k.astype(BF16)
        kv[here, inner:2 * inner] = (dot(y, wqkv[2]) * lax.rsqrt(mean_square + EPS)).astype(BF16)
        copies = []
        for i in range(1, seqs // 2):
            copies.append(gather_copy(kv, send, recv, i, seq, lax.rem(seq + 2 * i, seqs)))
        copies.append(gather_copy(kv, send, recv, 0, seq, sibling))
        for copy in copies:
            copy.start()
        q = dot(y, wqkv[0])
        for i in range(1, seqs // 2):
            source = lax.rem(seq + 2 * i, seqs)
            copy = gather_copy(kv, send, recv, seqs // 2 + i, source, sibling)
            copy.wait_recv()
            copy.start()
            copies.append(copy)
        gather_copy(kv, send, recv, 0, sibling, sibling).wait_recv()
        for i in range(1, seqs // 2):
            gather_copy(kv, send, recv, 0, lax.rem(sibling + 2 * i, seqs), sibling).wait_recv()
        for copy in copies:
            copy.wait_send()
        mix = mix_heads(q, mean_square, qk_ref[0:1, :], kv, seq * rows)
        return x, dot(mix, wo[...])

    def whole(src, dst, sems, target):
        return pltpu.make_async_remote_copy(
            src_ref=src, dst_ref=dst, send_sem=sems.at[0], recv_sem=sems.at[1],
            device_id={"layer": target}, device_id_type=MESH)

    def piece(src, dst, send, recv, c, target):
        at = pl.ds(pl.multiple_of(c * CHUNK, CHUNK), CHUNK)
        return pltpu.make_async_remote_copy(
            src_ref=src.at[at], dst_ref=dst.at[at], send_sem=send.at[c], recv_sem=recv.at[c],
            device_id={"layer": target}, device_id_type=MESH)

    def each_chunk(body):
        def step(c, carry):
            body(c)
            return carry
        lax.fori_loop(0, chunks, step, 0)

    @pl.when(even)
    def _():
        xs[...] = x_ref[...].astype(F32)

    @pl.when(odd)
    def _():
        whole(fine_out, fine_in, fine_sem, layer - 1).wait_recv()
        xs[...] = fine_in[...].astype(F32)

    x, branch = exact(kv_held, ga_send, ga_recv)
    fine_out[...] = (x + branch).astype(BF16)
    base[...] = -(x + 2.0 * branch)

    @pl.when(even)
    def _():
        copy = whole(fine_out, fine_in, fine_sem, layer + 1)
        copy.start()
        copy.wait_send()

    @pl.when(layer <= 1)
    def _():
        out_ref[...] = fine_out[...]

    @pl.when(layer == 1)
    def _():
        each_chunk(lambda c: piece(fine_out, cin, c_send, c_recv, c, layer + 1).start())
        each_chunk(lambda c: piece(fine_out, cin, c_send, c_recv, c, layer + 1).wait_send())

    @pl.when(jnp.logical_and(odd, layer > 1))
    def _():
        copy = whole(fine_out, term_in, term_sem, layer - 1)
        copy.start()
        copy.wait_send()

    @pl.when(jnp.logical_and(even, layer > 0))
    def _():
        whole(fine_out, term_in, term_sem, layer + 1).wait_recv()
        base[...] = base[...] + term_in[...].astype(F32)

        def advance(c):
            piece(cout, cin, c_send, c_recv, c, layer - 1).wait_recv()
            at = pl.ds(pl.multiple_of(c * CHUNK, CHUNK), CHUNK)
            x = cin[at, :].astype(F32)
            xs[at, :] = x
            mean_square = jnp.mean(x * x, axis=-1, keepdims=True)
            q = dot((x * gain_ref[...]).astype(BF16), wqkv[0])
            mix = mix_heads(q, mean_square, qk_ref[0:1, :], kv_held, seq * rows + c * CHUNK)
            cout[at, :] = (x + 2.0 * dot(mix, wo[...]) + base[at, :]).astype(BF16)

            @pl.when(layer < layers - 2)
            def _():
                piece(cout, cin, c_send, c_recv, c, layer + 2).start()

            piece(cout, nxt, n_send, n_recv, c, layer + 1).start()

        each_chunk(advance)
        x, branch = exact(kv_last, gb_send, gb_recv)
        out_ref[...] = (x + branch).astype(BF16)

        @pl.when(layer < layers - 2)
        def _():
            each_chunk(lambda c: piece(cout, cin, c_send, c_recv, c, layer + 2).wait_send())

        each_chunk(lambda c: piece(cout, nxt, n_send, n_recv, c, layer + 1).wait_send())

    @pl.when(jnp.logical_and(odd, layer > 1))
    def _():
        each_chunk(lambda c: piece(cout, nxt, n_send, n_recv, c, layer - 1).wait_recv())
        out_ref[...] = nxt[...]


def solution(mesh):
    layers, seqs = mesh.shape["layer"], mesh.shape["seq"]

    def on_device(states, w_qkv, w_out, norm_gain, qk_gain):
        rows, width = states.shape[1:]
        inner = w_out.shape[1]
        gains = jnp.tile(qk_gain[0], (1, inner // HEAD))
        vmem = pl.BlockSpec(memory_space=pltpu.VMEM)
        dma = pltpu.SemaphoreType.DMA
        state = pltpu.VMEM((rows, width), BF16)
        wide = pltpu.VMEM((rows, width), F32)
        gathered = pltpu.VMEM((rows * seqs, 2 * inner), BF16)
        out = pl.pallas_call(
            functools.partial(kernel, layers, seqs),
            out_shape=jax.ShapeDtypeStruct((rows, width), BF16),
            in_specs=[vmem] * 5,
            out_specs=vmem,
            scratch_shapes=[
                gathered, gathered, wide, wide, state, state, state, state, state, state,
                dma((seqs,)), dma((seqs,)), dma((seqs,)), dma((seqs,)), dma((2,)), dma((2,)),
                dma((rows // CHUNK,)), dma((rows // CHUNK,)), dma((rows // CHUNK,)), dma((rows // CHUNK,)),
            ],
            compiler_params=pltpu.CompilerParams(
                collective_id=0, has_side_effects=True, vmem_limit_bytes=56 << 20),
        )(states[0], w_qkv[0], w_out[0], norm_gain, gains)
        return out[None]

    in_specs = (
        P("layer", "seq", None),
        P("layer", None, None, None),
        P("layer", None, None),
        P("layer", None),
        P("layer", None, None),
    )
    return jax.shard_map(
        on_device, mesh=mesh, in_specs=in_specs, out_specs=P("layer", "seq", None), check_vma=False
    )
```

```python
import functools

import jax
import jax.numpy as jnp
from jax import lax
from jax.experimental import pallas as pl
from jax.experimental.pallas import tpu as pltpu
from jax.sharding import PartitionSpec as P

EPS = 1e-06
MESH = pl.DeviceIdType.MESH
F32 = jnp.float32
BF16 = jnp.bfloat16
NT = (((1,), (1,)), ((), ()))
LOG2E = 1.4426950408889634
HEAD = 64
PACK = 4
MEMBERS = 4
GROUP = 2 * MEMBERS
QUARTERS = 4


def dot(a, b):
    return jnp.dot(a, b, preferred_element_type=F32)


def spread_queries(q, mean_square, gain):
    rows, width = q.shape
    heads = width // HEAD
    row_head = lax.broadcasted_iota(jnp.int32, (heads, rows, width), 0)
    col_head = lax.broadcasted_iota(jnp.int32, (heads, rows, width), 2) // HEAD
    spread = jnp.where(row_head == col_head, q[None], 0.0)
    head_square = jnp.sum(spread * spread, axis=-1, keepdims=True) / HEAD
    scale = lax.rsqrt(head_square + EPS * (mean_square[None] + EPS)) * (LOG2E / 8.0)
    packed = (spread * gain).astype(BF16).reshape(heads * rows, width)
    return packed, scale.reshape(heads * rows, 1)


def mix_heads(q, mean_square, gain, columns, first_position):
    rows, width = q.shape
    packed, scale = spread_queries(q, mean_square, gain)
    many, wide = PACK * rows, PACK * HEAD
    outs = []
    for g in range(width // wide):
        these = slice(g * many, (g + 1) * many)
        keys = columns(g * wide, wide)
        tokens = keys.shape[0]
        scores = lax.dot_general(
            packed[these, g * wide:(g + 1) * wide], keys, NT, preferred_element_type=F32
        ) * scale[these]
        key_at = lax.broadcasted_iota(jnp.int32, (PACK, rows, tokens), 2).reshape(many, tokens)
        query_at = lax.broadcasted_iota(jnp.int32, (PACK, rows, tokens), 1).reshape(many, tokens)
        weights = jnp.where(key_at <= query_at + first_position, jnp.exp2(scores), 0.0)
        total = jnp.sum(weights, axis=-1, keepdims=True)
        mixed = dot(weights.astype(BF16), columns(width + g * wide, wide))
        mixed = (mixed * (1.0 / total)).reshape(PACK, rows, wide)
        row_head = lax.broadcasted_iota(jnp.int32, (PACK, rows, wide), 0)
        col_head = lax.broadcasted_iota(jnp.int32, (PACK, rows, wide), 2) // HEAD
        outs.append(jnp.sum(jnp.where(row_head == col_head, mixed, 0.0), axis=0).astype(BF16))
    return jnp.concatenate(outs, axis=-1)


def kernel(layers, seqs, x_hbm, wqkv_hbm, wo_hbm, gain_hbm, qk_hbm, out_ref,
           wq_all, wo_all, kv_all, kv_last, wkv, x_in, fine_in, cin, nxt, fine_out, guess_out,
           guess_all, term_all, chain, gains_all, qk_raw, gain_raw, xs, ys,
           load, gather_send, gather_recv, spread_send, spread_recv,
           fine_send, fine_recv, guess_send, guess_recv, term_send, term_recv,
           cin_send, cin_recv, nxt_send, nxt_recv, hop_sem, gain_send, gain_recv):
    layer = lax.axis_index("layer")
    seq = lax.axis_index("seq")
    units, unit, width = x_in.shape
    inner = width // 2
    group = layer // GROUP
    inside = lax.rem(layer, GROUP)
    member = inside // 2
    core = lax.rem(seq, 2)
    side = lax.rem(seq // 2, 2)
    even = lax.rem(layer, 2) == 0
    odd = jnp.logical_not(even)
    sibling = seq + 1 - 2 * core
    right, left = lax.rem(seq + 2, seqs), lax.rem(seq + seqs - 2, seqs)
    across = lax.rem(seq + 4, seqs)
    groups = layers // GROUP

    barrier = pltpu.get_barrier_semaphore()
    for other in (sibling, right, left):
        pl.semaphore_signal(barrier, inc=1, device_id={"seq": other}, device_id_type=MESH)
    for step in range(1, GROUP):
        other = group * GROUP + lax.rem(inside + step, GROUP)
        pl.semaphore_signal(barrier, inc=1, device_id={"layer": other}, device_id_type=MESH)

    @pl.when(group > 0)
    def _():
        pl.semaphore_signal(barrier, inc=1, device_id={"layer": layer - GROUP}, device_id_type=MESH)

    @pl.when(group < groups - 1)
    def _():
        pl.semaphore_signal(barrier, inc=1, device_id={"layer": layer + GROUP}, device_id_type=MESH)

    greeted = 3 + GROUP - 1 + jnp.where(group > 0, 1, 0) + jnp.where(group < groups - 1, 1, 0)

    loads = [
        pltpu.make_async_copy(x_hbm, x_in, load.at[0]),
        pltpu.make_async_copy(gain_hbm, gain_raw, load.at[1]),
        pltpu.make_async_copy(qk_hbm, qk_raw, load.at[2]),
        pltpu.make_async_copy(wqkv_hbm.at[1], wkv.at[0], load.at[3]),
        pltpu.make_async_copy(wqkv_hbm.at[2], wkv.at[1], load.at[4]),
        pltpu.make_async_copy(wqkv_hbm.at[0], wq_all.at[member], load.at[5]),
        pltpu.make_async_copy(wo_hbm, wo_all.at[member], load.at[6]),
    ]
    for copy in loads:
        copy.start()
    for copy in loads[:3]:
        copy.wait()
    gains_all[member, 0:1, :] = gain_raw[...]
    gains_all[member, 1:2, :] = jnp.concatenate([qk_raw[0:1, :]] * (inner // HEAD) + [qk_raw[1:2, :]] * (inner // HEAD), axis=-1)
    for copy in loads[3:]:
        copy.wait()
    norm_gain = gains_all[member, 0:1, :]
    query_gain = gains_all[member, 1:2, 0:inner]
    key_gain = gains_all[member, 1:2, inner:width]

    def remote(src, dst, send, recv, **target):
        return pltpu.make_async_remote_copy(
            src_ref=src, dst_ref=dst, send_sem=send, recv_sem=recv, device_id=target, device_id_type=MESH)

    def member_layer(m):
        return group * GROUP + 2 * m

    mine, others = 2 * side + core, 2 * (1 - side) + core
    sent = []

    def part(m, quarter, p):
        if p == 0:
            return wq_all.at[m, quarter]
        if p == 1:
            return wo_all.at[m, quarter]
        return kv_all.at[m, 2 * quarter + p - 2]

    def spread_copy(slot, m, quarter, p, **target):
        ref = part(m, quarter, p)
        return remote(ref, ref, spread_send.at[slot], spread_recv.at[m, quarter, p], **target)

    def hand(m, quarter, p, **target):
        copy = spread_copy(len(sent), m, quarter, p, **target)
        copy.start()
        sent.append(copy)

    def await_part(m, quarter, p):
        spread_copy(0, m, quarter, p, seq=sibling).wait_recv()

    def nth(step):
        return lax.rem(member + step + MEMBERS, MEMBERS)

    def spread_first(parts):
        for p in parts:
            hand(member, mine, p, layer=member_layer(nth(1)))
            hand(member, mine, p, layer=member_layer(nth(-1)))

    def spread_near(parts):
        for p in parts:
            for step in (-1, 1):
                m = nth(step)
                await_part(m, mine, p)
                if step == -1 and p % 2 == 0:
                    hand(m, mine, p, layer=member_layer(nth(1)))
                if step == 1 and p % 2 == 1:
                    hand(m, mine, p, layer=member_layer(nth(-1)))
                hand(m, mine, p, seq=right if p % 2 == 0 else left)
                hand(m, mine, p, seq=sibling)

    def spread_far(parts):
        for p in parts:
            m = nth(2)
            await_part(m, mine, p)
            hand(m, mine, p, seq=right if p % 2 == 0 else left)
            hand(m, mine, p, seq=sibling)

    def spread_side(parts, steps):
        for step in steps:
            for p in parts:
                m = nth(step)
                await_part(m, others, p)
                hand(m, others, p, seq=sibling)

    def exact(source, ready, kv, send, recv, between):
        copies = []

        def at(block, u):
            return kv(block).at[pl.ds(u * unit, unit)]

        def push(block, u, target):
            copy = remote(at(block, u), at(block, u), send.at[len(copies)], recv.at[block, u], seq=target)
            copy.start()
            copies.append(copy)

        def arrived(block, u):
            remote(at(block, u), at(block, u), send.at[0], recv.at[block, u], seq=sibling).wait_recv()

        same = lax.broadcasted_iota(jnp.int32, (inner, inner), 0) // HEAD
        same = (same == lax.broadcasted_iota(jnp.int32, (inner, inner), 1) // HEAD).astype(BF16)
        for u in range(units):
            ready(u)
            here = pl.ds(u * unit, unit)
            x = source[u].astype(F32)
            xs[here, :] = x
            mean_square = jnp.mean(x * x, axis=-1, keepdims=True)
            y = (x * norm_gain).astype(BF16)
            ys[here, :] = y
            k = dot(y, wkv[0].reshape(width, inner))
            head_square = dot((k * k).astype(BF16), same) / HEAD
            k = k * lax.rsqrt(head_square + EPS * (mean_square + EPS)) * key_gain
            at(seq, u)[:, 0:inner] = k.astype(BF16)
            at(seq, u)[:, inner:width] = (dot(y, wkv[1].reshape(width, inner)) * lax.rsqrt(mean_square + EPS)).astype(BF16)
            if u == 0:
                between()
            push(seq, u, right)
            push(seq, u, left)
            push(seq, u, sibling)
        for u in range(units):
            arrived(left, u)
            if u % 2 == 0:
                push(left, u, right)
            push(left, u, sibling)
            arrived(right, u)
            if u % 2 == 1:
                push(right, u, left)
            push(right, u, sibling)
        for u in range(units):
            arrived(across, u)
            push(across, u, sibling)
        for step in (0, 2, 6, 4):
            for u in range(units):
                arrived(lax.rem(sibling + step, seqs), u)
        x = xs[...]
        mean_square = jnp.mean(x * x, axis=-1, keepdims=True)
        q = dot(ys[...], wq_all[member].reshape(width, inner))

        def columns(start, size):
            return kv(slice(None))[:, :, start:start + size].reshape(seqs * units * unit, size)

        mix = mix_heads(q, mean_square, query_gain, columns, seq * units * unit)
        branch = dot(mix, wo_all[member].reshape(inner, width))
        return x, branch, copies

    def held(block):
        return kv_all.at[member, block]

    def last(block):
        return kv_last.at[block]

    def fine_copy(u, target):
        return remote(fine_out.at[u], fine_in.at[u], fine_send.at[u], fine_recv.at[u], layer=target)

    @pl.when(even)
    def _():
        for u in range(units):
            fine_in[u] = x_in[u]

    def fine_ready(u):
        @pl.when(odd)
        def _():
            if u == 0:
                pl.semaphore_wait(barrier, greeted)
            fine_copy(u, layer - 1).wait_recv()

    def meet():
        @pl.when(even)
        def _():
            pl.semaphore_wait(barrier, greeted)

    def gain_copy(step):
        ref = gains_all.at[member]
        return remote(ref, ref, gain_send.at[step - 1], gain_recv.at[member], layer=member_layer(nth(step)))

    x, branch, copies = exact(fine_in, fine_ready, held, gather_send.at[0], gather_recv.at[0], meet)
    fine_out[...] = (x + branch).astype(BF16).reshape(units, unit, width)

    def guess_copy(u, m):
        return remote(guess_out.at[u], guess_all.at[m], guess_send.at[u], guess_recv.at[m], layer=member_layer(u))

    def term_copy(u):
        return remote(fine_out.at[u], term_all.at[member], term_send.at[u], term_recv.at[member], layer=member_layer(u))

    def start_copy(u):
        return remote(fine_out.at[u], chain.at[0], term_send.at[u], hop_sem.at[1], layer=member_layer(u))

    @pl.when(odd)
    def _():
        @pl.when(layer == 1)
        def _():
            for u in range(units):
                start_copy(u).start()
            out_ref[...] = fine_out[...]

        @pl.when(layer > 1)
        def _():
            for u in range(units):
                term_copy(u).start()

        for copy in copies:
            copy.wait_send()
        for u in range(units):
            term_copy(u).wait_send()

        @pl.when(layer > 1)
        def _():
            for u in range(units):
                remote(chain.at[0], nxt.at[u], nxt_send.at[0], nxt_recv.at[u], layer=layer - 1).wait_recv()
            out_ref[...] = nxt[...]

    @pl.when(even)
    def _():
        for u in range(units):
            fine_copy(u, layer + 1).start()
        guess_out[...] = (x + 2.0 * branch).astype(BF16).reshape(units, unit, width)
        for u in range(units):
            @pl.when(jnp.logical_and(u != member, layer > 0))
            def _():
                guess_copy(u, member).start()
        guess_all[member] = guess_out[member]
        for step in (1, 2, 3):
            gain_copy(step).start()
        spread_first((0, 1))
        spread_first((2, 3))
        spread_near((0, 1))
        spread_far((0, 1))
        spread_near((2, 3))
        spread_side((0, 1), (-1, 1, 2))
        spread_far((2, 3))
        spread_side((2, 3), (-1, 1, 2))
        for step in (1, 2, 3):
            m = nth(step)
            for p in range(4):
                await_part(m, 2 * side + 1 - core, p)
                await_part(m, 2 * (1 - side) + 1 - core, p)
            remote(gains_all.at[m], gains_all.at[m], gain_send.at[0], gain_recv.at[m], seq=sibling).wait_recv()

        def cin_copy(m):
            return remote(chain.at[m], cin.at[member], cin_send.at[m], cin_recv.at[member], layer=member_layer(m))

        def nxt_copy(m):
            return remote(chain.at[m + 1], nxt.at[member], nxt_send.at[m], nxt_recv.at[member], layer=member_layer(m) + 1)

        def hop_copy(target):
            return remote(chain.at[MEMBERS], chain.at[0], hop_sem.at[0], hop_sem.at[1], layer=target)

        hop_copy(lax.rem(layer + GROUP, layers)).wait_recv()

        def advance(m, carry):
            first = jnp.logical_and(group == 0, m == 0)

            @pl.when(first)
            def _():
                chain[m + 1] = chain[m]

            @pl.when(jnp.logical_not(first))
            def _():
                @pl.when(m != member)
                def _():
                    cin_copy(m).start()
                    remote(guess_out.at[0], guess_all.at[m], guess_send.at[0], guess_recv.at[m], layer=layer + 1).wait_recv()

                @pl.when(m == member)
                def _():
                    cin[member] = chain[m]

                remote(fine_out.at[0], term_all.at[m], term_send.at[0], term_recv.at[m], layer=layer + 1).wait_recv()
                x = chain[m].astype(F32)
                mean_square = jnp.mean(x * x, axis=-1, keepdims=True)
                q = dot((x * gains_all[m, 0:1, :]).astype(BF16), wq_all[m].reshape(width, inner))

                def columns(start, size):
                    return kv_all[m, :, :, start:start + size].reshape(seqs * units * unit, size)

                mix = mix_heads(q, mean_square, gains_all[m, 1:2, 0:inner], columns, (seq * units + member) * unit)
                branch = dot(mix, wo_all[m].reshape(inner, width))
                correction = term_all[m].astype(F32) - guess_all[m].astype(F32)
                chain[m + 1] = (x + 2.0 * branch + correction).astype(BF16)
                nxt_copy(m).start()

            return carry

        lax.fori_loop(0, MEMBERS, advance, 0)

        @pl.when(group < groups - 1)
        def _():
            hop_copy(layer + GROUP).start()

        def cin_ready(u):
            @pl.when(u != member)
            def _():
                remote(chain.at[0], cin.at[u], cin_send.at[0], cin_recv.at[u], layer=layer + 1).wait_recv()

        @pl.when(layer == 0)
        def _():
            out_ref[...] = fine_out[...]

        @pl.when(layer > 0)
        def _():
            x, branch, more = exact(cin, cin_ready, last, gather_send.at[1], gather_recv.at[1], lambda: None)
            out_ref[...] = (x + branch).astype(BF16).reshape(units, unit, width)
            for copy in more:
                copy.wait_send()

        for copy in copies:
            copy.wait_send()
        for copy in sent:
            copy.wait_send()
        for step in (1, 2, 3):
            gain_copy(step).wait_send()
        for u in range(units):
            fine_copy(u, layer + 1).wait_send()

            @pl.when(jnp.logical_and(u != member, layer > 0))
            def _():
                guess_copy(u, member).wait_send()

        def drain(m, carry):
            @pl.when(jnp.logical_not(jnp.logical_and(group == 0, m == 0)))
            def _():
                nxt_copy(m).wait_send()

                @pl.when(m != member)
                def _():
                    cin_copy(m).wait_send()

            return carry

        lax.fori_loop(0, MEMBERS, drain, 0)

        @pl.when(group < groups - 1)
        def _():
            hop_copy(layer + GROUP).wait_send()


def solution(mesh):
    layers, seqs = mesh.shape["layer"], mesh.shape["seq"]

    def on_device(states, w_qkv, w_out, norm_gain, qk_gain):
        rows, width = states.shape[1:]
        inner = w_out.shape[1]
        unit = rows // MEMBERS
        hbm = pl.BlockSpec(memory_space=pl.ANY)
        dma = pltpu.SemaphoreType.DMA
        state = pltpu.VMEM((MEMBERS, unit, width), BF16)
        out = pl.pallas_call(
            functools.partial(kernel, layers, seqs),
            out_shape=jax.ShapeDtypeStruct((MEMBERS, unit, width), BF16),
            in_specs=[hbm] * 5,
            out_specs=pl.BlockSpec(memory_space=pltpu.VMEM),
            scratch_shapes=[
                pltpu.VMEM((MEMBERS, QUARTERS, width // QUARTERS, inner), BF16),
                pltpu.VMEM((MEMBERS, QUARTERS, inner // QUARTERS, width), BF16),
                pltpu.VMEM((MEMBERS, seqs, rows, 2 * inner), BF16),
                pltpu.VMEM((seqs, rows, 2 * inner), BF16),
                pltpu.VMEM((2, QUARTERS, width // QUARTERS, inner), BF16),
                state, state, state, state, state, state, state, state,
                pltpu.VMEM((MEMBERS + 1, unit, width), BF16),
                pltpu.VMEM((MEMBERS, 8, width), F32),
                pltpu.VMEM((2, HEAD), F32),
                pltpu.VMEM((1, width), F32),
                pltpu.VMEM((rows, width), F32),
                pltpu.VMEM((rows, width), BF16),
                dma((7,)), dma((2, 28)), dma((2, seqs, MEMBERS)), dma((48,)), dma((MEMBERS, QUARTERS, 4)),
                dma((4,)), dma((4,)), dma((4,)), dma((4,)), dma((4,)), dma((4,)),
                dma((4,)), dma((4,)), dma((4,)), dma((4,)), dma((2,)), dma((3,)), dma((4,)),
            ],
            compiler_params=pltpu.CompilerParams(
                collective_id=0, has_side_effects=True, vmem_limit_bytes=56 << 20),
        )(
            states.reshape(MEMBERS, unit, width),
            w_qkv.reshape(3, QUARTERS, width // QUARTERS, inner),
            w_out.reshape(QUARTERS, inner // QUARTERS, width),
            norm_gain, qk_gain[0],
        )
        return out.reshape(1, rows, width)

    in_specs = (
        P("layer", "seq", None),
        P("layer", None, None, None),
        P("layer", None, None),
        P("layer", None),
        P("layer", None, None),
    )
    return jax.shard_map(
        on_device, mesh=mesh, in_specs=in_specs, out_specs=P("layer", "seq", None), check_vma=False
    )
```

```python
import functools

import jax
import jax.numpy as jnp
from jax import lax
from jax.experimental import pallas as pl
from jax.experimental.pallas import tpu as pltpu
from jax.sharding import PartitionSpec as P

EPS = 1e-06
MESH = pl.DeviceIdType.MESH
F32 = jnp.float32
BF16 = jnp.bfloat16
NT = (((1,), (1,)), ((), ()))
LOG2E = 1.4426950408889634
HEAD = 64
PACK = 4
MEMBERS = 4
GROUP = 2 * MEMBERS
QUARTERS = 4


def dot(a, b):
    return jnp.dot(a, b, preferred_element_type=F32)


def spread_queries(q, mean_square, gain):
    rows, width = q.shape
    heads = width // HEAD
    row_head = lax.broadcasted_iota(jnp.int32, (heads, rows, width), 0)
    col_head = lax.broadcasted_iota(jnp.int32, (heads, rows, width), 2) // HEAD
    spread = jnp.where(row_head == col_head, q[None], 0.0)
    head_square = jnp.sum(spread * spread, axis=-1, keepdims=True) / HEAD
    scale = lax.rsqrt(head_square + EPS * (mean_square[None] + EPS)) * (LOG2E / 8.0)
    packed = (spread * gain).astype(BF16).reshape(heads * rows, width)
    return packed, scale.reshape(heads * rows, 1)


def mix_heads(q, mean_square, gain, columns, first_position):
    rows, width = q.shape
    packed, scale = spread_queries(q, mean_square, gain)
    many, wide = PACK * rows, PACK * HEAD
    outs = []
    for g in range(width // wide):
        these = slice(g * many, (g + 1) * many)
        keys = columns(g * wide, wide)
        tokens = keys.shape[0]
        scores = lax.dot_general(
            packed[these, g * wide:(g + 1) * wide], keys, NT, preferred_element_type=F32
        ) * scale[these]
        key_at = lax.broadcasted_iota(jnp.int32, (PACK, rows, tokens), 2).reshape(many, tokens)
        query_at = lax.broadcasted_iota(jnp.int32, (PACK, rows, tokens), 1).reshape(many, tokens)
        weights = jnp.where(key_at <= query_at + first_position, jnp.exp2(scores), 0.0)
        total = jnp.sum(weights, axis=-1, keepdims=True)
        mixed = dot(weights.astype(BF16), columns(width + g * wide, wide))
        mixed = (mixed * (1.0 / total)).reshape(PACK, rows, wide)
        row_head = lax.broadcasted_iota(jnp.int32, (PACK, rows, wide), 0)
        col_head = lax.broadcasted_iota(jnp.int32, (PACK, rows, wide), 2) // HEAD
        outs.append(jnp.sum(jnp.where(row_head == col_head, mixed, 0.0), axis=0).astype(BF16))
    return jnp.concatenate(outs, axis=-1)


def kernel(layers, seqs, x_hbm, wqkv_hbm, wo_hbm, gain_hbm, qk_hbm, out_ref,
           wq_all, wo_all, kv_all, kv_last, wkv, x_in, fine_in, cin, nxt, fine_out, guess_out,
           guess_all, term_all, chain, gains_all, qk_raw, gain_raw, xs, ys,
           load, gather_send, gather_recv, spread_send, spread_recv,
           fine_send, fine_recv, guess_send, guess_recv, term_send, term_recv,
           cin_send, cin_recv, nxt_send, nxt_recv, hop_sem, gain_send, gain_recv):
    layer = lax.axis_index("layer")
    seq = lax.axis_index("seq")
    units, unit, width = x_in.shape
    inner = width // 2
    group = layer // GROUP
    inside = lax.rem(layer, GROUP)
    member = inside // 2
    core = lax.rem(seq, 2)
    side = lax.rem(seq // 2, 2)
    even = lax.rem(layer, 2) == 0
    odd = jnp.logical_not(even)
    sibling = seq + 1 - 2 * core
    right, left = lax.rem(seq + 2, seqs), lax.rem(seq + seqs - 2, seqs)
    across = lax.rem(seq + 4, seqs)
    groups = layers // GROUP

    barrier = pltpu.get_barrier_semaphore()
    for other in (sibling, right, left):
        pl.semaphore_signal(barrier, inc=1, device_id={"seq": other}, device_id_type=MESH)
    for step in range(1, GROUP):
        other = group * GROUP + lax.rem(inside + step, GROUP)
        pl.semaphore_signal(barrier, inc=1, device_id={"layer": other}, device_id_type=MESH)

    @pl.when(group > 0)
    def _():
        pl.semaphore_signal(barrier, inc=1, device_id={"layer": layer - GROUP}, device_id_type=MESH)

    @pl.when(group < groups - 1)
    def _():
        pl.semaphore_signal(barrier, inc=1, device_id={"layer": layer + GROUP}, device_id_type=MESH)

    greeted = 3 + GROUP - 1 + jnp.where(group > 0, 1, 0) + jnp.where(group < groups - 1, 1, 0)

    loads = [
        pltpu.make_async_copy(x_hbm, x_in, load.at[0]),
        pltpu.make_async_copy(gain_hbm, gain_raw, load.at[1]),
        pltpu.make_async_copy(qk_hbm, qk_raw, load.at[2]),
        pltpu.make_async_copy(wqkv_hbm.at[1], wkv.at[0], load.at[3]),
        pltpu.make_async_copy(wqkv_hbm.at[2], wkv.at[1], load.at[4]),
        pltpu.make_async_copy(wqkv_hbm.at[0], wq_all.at[member], load.at[5]),
        pltpu.make_async_copy(wo_hbm, wo_all.at[member], load.at[6]),
    ]
    for copy in loads:
        copy.start()
    for copy in loads[:3]:
        copy.wait()
    gains_all[member, 0:1, :] = gain_raw[...]
    gains_all[member, 1:2, :] = jnp.concatenate([qk_raw[0:1, :]] * (inner // HEAD) + [qk_raw[1:2, :]] * (inner // HEAD), axis=-1)
    for copy in loads[3:]:
        copy.wait()
    norm_gain = gains_all[member, 0:1, :]
    query_gain = gains_all[member, 1:2, 0:inner]
    key_gain = gains_all[member, 1:2, inner:width]

    def remote(src, dst, send, recv, **target):
        return pltpu.make_async_remote_copy(
            src_ref=src, dst_ref=dst, send_sem=send, recv_sem=recv, device_id=target, device_id_type=MESH)

    def member_layer(m):
        return group * GROUP + 2 * m

    mine, others = 2 * side + core, 2 * (1 - side) + core
    sent = []

    def part(m, quarter, p):
        if p == 0:
            return wq_all.at[m, quarter]
        if p == 1:
            return wo_all.at[m, quarter]
        return kv_all.at[m, 2 * quarter + p - 2]

    def spread_copy(slot, m, quarter, p, **target):
        ref = part(m, quarter, p)
        return remote(ref, ref, spread_send.at[slot], spread_recv.at[m, quarter, p], **target)

    def hand(m, quarter, p, **target):
        spread_copy(len(sent), m, quarter, p, **target).start()
        sent.append(p)

    def await_part(m, quarter, p):
        spread_copy(0, m, quarter, p, seq=sibling).wait_recv()

    def nth(step):
        return lax.rem(member + step + MEMBERS, MEMBERS)

    def spread_first(step, parts):
        for p in parts:
            hand(member, mine, p, layer=member_layer(nth(step)))

    def spread_near(step, p):
        m = nth(step)
        await_part(m, mine, p)
        if (step == -1) == (p % 2 == 0):
            hand(m, mine, p, layer=member_layer(nth(-step)))
        hand(m, mine, p, seq=right if p % 2 == 0 else left)
        hand(m, mine, p, seq=sibling)

    def spread_far(p):
        m = nth(2)
        await_part(m, mine, p)
        hand(m, mine, p, seq=right if p % 2 == 0 else left)
        hand(m, mine, p, seq=sibling)

    def spread_side(step, p):
        m = nth(step)
        await_part(m, others, p)
        hand(m, others, p, seq=sibling)

    def exact(source, ready, kv, send, recv, meet, pushed, gathered):
        copies = []

        def at(block, u):
            return kv(block).at[pl.ds(u * unit, unit)]

        def push(block, u, target):
            copy = remote(at(block, u), at(block, u), send.at[len(copies)], recv.at[block, u], seq=target)
            copy.start()
            copies.append(copy)

        def arrived(block, u):
            remote(at(block, u), at(block, u), send.at[0], recv.at[block, u], seq=sibling).wait_recv()

        same = lax.broadcasted_iota(jnp.int32, (inner, inner), 0) // HEAD
        same = (same == lax.broadcasted_iota(jnp.int32, (inner, inner), 1) // HEAD).astype(BF16)
        for u in range(units):
            ready(u)
            here = pl.ds(u * unit, unit)
            x = source[u].astype(F32)
            xs[here, :] = x
            mean_square = jnp.mean(x * x, axis=-1, keepdims=True)
            y = (x * norm_gain).astype(BF16)
            ys[here, :] = y
            k = dot(y, wkv[0].reshape(width, inner))
            head_square = dot((k * k).astype(BF16), same) / HEAD
            k = k * lax.rsqrt(head_square + EPS * (mean_square + EPS)) * key_gain
            at(seq, u)[:, 0:inner] = k.astype(BF16)
            at(seq, u)[:, inner:width] = (dot(y, wkv[1].reshape(width, inner)) * lax.rsqrt(mean_square + EPS)).astype(BF16)
            if u == 0:
                meet()
            push(seq, u, right)
            push(seq, u, left)
            push(seq, u, sibling)
        pushed()
        for u in range(units):
            arrived(left, u)
            if u % 2 == 0:
                push(left, u, right)
            push(left, u, sibling)
            arrived(right, u)
            if u % 2 == 1:
                push(right, u, left)
            push(right, u, sibling)
        for u in range(units):
            arrived(across, u)
            push(across, u, sibling)
        for step in (0, 2, 6, 4):
            for u in range(units):
                arrived(lax.rem(sibling + step, seqs), u)
        gathered()
        x = xs[...]
        mean_square = jnp.mean(x * x, axis=-1, keepdims=True)
        q = dot(ys[...], wq_all[member].reshape(width, inner))

        def columns(start, size):
            return kv(slice(None))[:, :, start:start + size].reshape(seqs * units * unit, size)

        mix = mix_heads(q, mean_square, query_gain, columns, seq * units * unit)
        branch = dot(mix, wo_all[member].reshape(inner, width))
        return x, branch, copies

    def held(block):
        return kv_all.at[member, block]

    def last(block):
        return kv_last.at[block]

    def fine_copy(u, target):
        return remote(fine_out.at[u], fine_in.at[u], fine_send.at[u], fine_recv.at[u], layer=target)

    @pl.when(even)
    def _():
        for u in range(units):
            fine_in[u] = x_in[u]

    def fine_ready(u):
        @pl.when(odd)
        def _():
            if u == 0:
                pl.semaphore_wait(barrier, greeted)
            fine_copy(u, layer - 1).wait_recv()

    def meet():
        @pl.when(even)
        def _():
            pl.semaphore_wait(barrier, greeted)

    def pushed():
        @pl.when(even)
        def _():
            spread_first(1, (0, 1))
            spread_first(-1, (1, 0))
            for step in (1, 2, 3):
                gain_copy(step).start()

    def gathered():
        @pl.when(even)
        def _():
            spread_first(-1, (3, 2))
            spread_near(-1, 0)
            spread_near(1, 1)

    def nothing():
        pass

    def gain_copy(step):
        ref = gains_all.at[member]
        return remote(ref, ref, gain_send.at[step - 1], gain_recv.at[member], layer=member_layer(nth(step)))

    x, branch, copies = exact(fine_in, fine_ready, held, gather_send.at[0], gather_recv.at[0], meet, pushed, gathered)
    fine_out[...] = (x + branch).astype(BF16).reshape(units, unit, width)

    def guess_copy(u, m):
        return remote(guess_out.at[u], guess_all.at[m], guess_send.at[u], guess_recv.at[m], layer=member_layer(u))

    def term_copy(u):
        return remote(fine_out.at[u], term_all.at[member], term_send.at[u], term_recv.at[member], layer=member_layer(u))

    def start_copy(u):
        return remote(fine_out.at[u], chain.at[0], term_send.at[u], hop_sem.at[1], layer=member_layer(u))

    @pl.when(odd)
    def _():
        @pl.when(layer == 1)
        def _():
            for u in range(units):
                start_copy(u).start()
            out_ref[...] = fine_out[...]

        @pl.when(layer > 1)
        def _():
            for u in range(units):
                term_copy(u).start()

        for copy in copies:
            copy.wait_send()
        for u in range(units):
            term_copy(u).wait_send()

        @pl.when(layer > 1)
        def _():
            for u in range(units):
                remote(chain.at[0], nxt.at[u], nxt_send.at[0], nxt_recv.at[u], layer=layer - 1).wait_recv()
            out_ref[...] = nxt[...]

    @pl.when(even)
    def _():
        for u in range(units):
            fine_copy(u, layer + 1).start()
        spread_near(-1, 1)
        spread_near(1, 0)
        guess_out[...] = (x + 2.0 * branch).astype(BF16).reshape(units, unit, width)
        for u in range(units):
            fine_copy(u, layer + 1).wait_send()
        spread_first(1, (2, 3))
        for u in range(units):
            @pl.when(jnp.logical_and(u != member, layer > 0))
            def _():
                guess_copy(u, member).start()
        guess_all[member] = guess_out[member]
        spread_side(-1, 0)
        spread_side(1, 1)
        spread_far(0)
        spread_far(1)
        spread_near(1, 3)
        spread_side(-1, 1)
        spread_side(1, 0)
        spread_near(1, 2)
        spread_near(-1, 2)
        spread_side(2, 0)
        spread_side(2, 1)
        spread_far(3)
        spread_side(1, 3)
        spread_near(-1, 3)
        spread_side(1, 2)
        spread_far(2)
        spread_side(-1, 2)
        spread_side(-1, 3)
        spread_side(2, 3)
        spread_side(2, 2)
        for step in (1, 2, 3):
            m = nth(step)
            for p in range(4):
                await_part(m, 2 * side + 1 - core, p)
                await_part(m, 2 * (1 - side) + 1 - core, p)
            remote(gains_all.at[m], gains_all.at[m], gain_send.at[0], gain_recv.at[m], seq=sibling).wait_recv()

        def cin_copy(m):
            return remote(chain.at[m], cin.at[member], cin_send.at[m], cin_recv.at[member], layer=member_layer(m))

        def nxt_copy(m):
            return remote(chain.at[m + 1], nxt.at[member], nxt_send.at[m], nxt_recv.at[member], layer=member_layer(m) + 1)

        def hop_copy(target):
            return remote(chain.at[MEMBERS], chain.at[0], hop_sem.at[0], hop_sem.at[1], layer=target)

        hop_copy(lax.rem(layer + GROUP, layers)).wait_recv()

        def advance(m, carry):
            first = jnp.logical_and(group == 0, m == 0)

            @pl.when(first)
            def _():
                chain[m + 1] = chain[m]

            @pl.when(jnp.logical_not(first))
            def _():
                @pl.when(m != member)
                def _():
                    cin_copy(m).start()
                    remote(guess_out.at[0], guess_all.at[m], guess_send.at[0], guess_recv.at[m], layer=layer + 1).wait_recv()

                @pl.when(m == member)
                def _():
                    cin[member] = chain[m]

                remote(fine_out.at[0], term_all.at[m], term_send.at[0], term_recv.at[m], layer=layer + 1).wait_recv()
                x = chain[m].astype(F32)
                mean_square = jnp.mean(x * x, axis=-1, keepdims=True)
                q = dot((x * gains_all[m, 0:1, :]).astype(BF16), wq_all[m].reshape(width, inner))

                def columns(start, size):
                    return kv_all[m, :, :, start:start + size].reshape(seqs * units * unit, size)

                mix = mix_heads(q, mean_square, gains_all[m, 1:2, 0:inner], columns, (seq * units + member) * unit)
                branch = dot(mix, wo_all[m].reshape(inner, width))
                correction = term_all[m].astype(F32) - guess_all[m].astype(F32)
                chain[m + 1] = (x + 2.0 * branch + correction).astype(BF16)
                nxt_copy(m).start()

            return carry

        lax.fori_loop(0, MEMBERS, advance, 0)

        @pl.when(group < groups - 1)
        def _():
            hop_copy(layer + GROUP).start()

        def cin_ready(u):
            @pl.when(u != member)
            def _():
                remote(chain.at[0], cin.at[u], cin_send.at[0], cin_recv.at[u], layer=layer + 1).wait_recv()

        @pl.when(layer == 0)
        def _():
            out_ref[...] = fine_out[...]

        @pl.when(layer > 0)
        def _():
            x, branch, more = exact(cin, cin_ready, last, gather_send.at[1], gather_recv.at[1], nothing, nothing, nothing)
            out_ref[...] = (x + branch).astype(BF16).reshape(units, unit, width)
            for copy in more:
                copy.wait_send()

        for copy in copies:
            copy.wait_send()
        for slot, p in enumerate(sent):
            spread_copy(slot, member, mine, p, seq=sibling).wait_send()
        for step in (1, 2, 3):
            gain_copy(step).wait_send()
        for u in range(units):
            @pl.when(jnp.logical_and(u != member, layer > 0))
            def _():
                guess_copy(u, member).wait_send()

        def drain(m, carry):
            @pl.when(jnp.logical_not(jnp.logical_and(group == 0, m == 0)))
            def _():
                nxt_copy(m).wait_send()

                @pl.when(m != member)
                def _():
                    cin_copy(m).wait_send()

            return carry

        lax.fori_loop(0, MEMBERS, drain, 0)

        @pl.when(group < groups - 1)
        def _():
            hop_copy(layer + GROUP).wait_send()


def solution(mesh):
    layers, seqs = mesh.shape["layer"], mesh.shape["seq"]

    def on_device(states, w_qkv, w_out, norm_gain, qk_gain):
        rows, width = states.shape[1:]
        inner = w_out.shape[1]
        unit = rows // MEMBERS
        hbm = pl.BlockSpec(memory_space=pl.ANY)
        dma = pltpu.SemaphoreType.DMA
        state = pltpu.VMEM((MEMBERS, unit, width), BF16)
        out = pl.pallas_call(
            functools.partial(kernel, layers, seqs),
            out_shape=jax.ShapeDtypeStruct((MEMBERS, unit, width), BF16),
            in_specs=[hbm] * 5,
            out_specs=pl.BlockSpec(memory_space=pltpu.VMEM),
            scratch_shapes=[
                pltpu.VMEM((MEMBERS, QUARTERS, width // QUARTERS, inner), BF16),
                pltpu.VMEM((MEMBERS, QUARTERS, inner // QUARTERS, width), BF16),
                pltpu.VMEM((MEMBERS, seqs, rows, 2 * inner), BF16),
                pltpu.VMEM((seqs, rows, 2 * inner), BF16),
                pltpu.VMEM((2, QUARTERS, width // QUARTERS, inner), BF16),
                state, state, state, state, state, state, state, state,
                pltpu.VMEM((MEMBERS + 1, unit, width), BF16),
                pltpu.VMEM((MEMBERS, 8, width), F32),
                pltpu.VMEM((2, HEAD), F32),
                pltpu.VMEM((1, width), F32),
                pltpu.VMEM((rows, width), F32),
                pltpu.VMEM((rows, width), BF16),
                dma((7,)), dma((2, 28)), dma((2, seqs, MEMBERS)), dma((48,)), dma((MEMBERS, QUARTERS, 4)),
                dma((4,)), dma((4,)), dma((4,)), dma((4,)), dma((4,)), dma((4,)),
                dma((4,)), dma((4,)), dma((4,)), dma((4,)), dma((2,)), dma((3,)), dma((4,)),
            ],
            compiler_params=pltpu.CompilerParams(
                collective_id=0, has_side_effects=True, vmem_limit_bytes=56 << 20),
        )(
            states.reshape(MEMBERS, unit, width),
            w_qkv.reshape(3, QUARTERS, width // QUARTERS, inner),
            w_out.reshape(QUARTERS, inner // QUARTERS, width),
            norm_gain, qk_gain[0],
        )
        return out.reshape(1, rows, width)

    in_specs = (
        P("layer", "seq", None),
        P("layer", None, None, None),
        P("layer", None, None),
        P("layer", None),
        P("layer", None, None),
    )
    return jax.shard_map(
        on_device, mesh=mesh, in_specs=in_specs, out_specs=P("layer", "seq", None), check_vma=False
    )
```

```python
import functools

import jax
import jax.numpy as jnp
from jax import lax
from jax.experimental import pallas as pl
from jax.experimental.pallas import tpu as pltpu
from jax.sharding import PartitionSpec as P

EPS = 1e-06
MESH = pl.DeviceIdType.MESH
F32 = jnp.float32
BF16 = jnp.bfloat16
NT = (((1,), (1,)), ((), ()))
LOG2E = 1.4426950408889634
HEAD = 64
PACK = 4
MEMBERS = 4
GROUP = 2 * MEMBERS
QUARTERS = 4
WEIGHT_PARTS = (0, 1, 2, 3)
STATE_PARTS = (4, 5, 6, 7)
ONWARD = (4, 5, 6)

FIRST_ORDER = (0, 1, 3, 2)
UNIT_ORDER = (0, 1, 3, 2)
EARLY = (("near", -1, 0), ("near", 1, 0), ("near", -1, 1), ("near", 1, 1), ("near", -1, 2), ("near", 1, 2))
LATE = (
    ("near", -1, 3), ("near", 1, 3), ("side", -1, 0), ("side", -1, 1), ("near", -1, 4), ("near", 1, 7),
    ("side", 1, 0), ("side", 1, 1), ("near", 1, 4), ("side", -1, 2), ("side", -1, 3), ("near", 1, 5),
    ("side", 1, 2), ("side", 1, 3), ("near", -1, 5), ("near", 1, 6), ("side", -1, 4), ("side", 1, 7),
    ("near", -1, 6), ("far", 2, 0), ("side", 1, 4), ("side", 1, 5), ("near", -1, 7), ("far", 2, 1),
    ("side", -1, 5), ("side", 1, 6), ("far", 2, 2), ("far", 2, 4), ("side", -1, 6), ("side", -1, 7),
    ("far", 2, 3), ("far", 2, 5), ("side", 2, 0), ("side", 2, 1), ("far", 2, 7), ("far", 2, 6),
    ("side", 2, 2), ("side", 2, 3), ("side", 2, 4), ("side", 2, 5), ("side", 2, 6), ("side", 2, 7),
)


def dot(a, b):
    return jnp.dot(a, b, preferred_element_type=F32)


def spread_queries(q, mean_square, gain):
    rows, width = q.shape
    heads = width // HEAD
    row_head = lax.broadcasted_iota(jnp.int32, (heads, rows, width), 0)
    col_head = lax.broadcasted_iota(jnp.int32, (heads, rows, width), 2) // HEAD
    spread = jnp.where(row_head == col_head, q[None], 0.0)
    head_square = jnp.sum(spread * spread, axis=-1, keepdims=True) / HEAD
    scale = lax.rsqrt(head_square + EPS * (mean_square[None] + EPS)) * (LOG2E / 8.0)
    packed = (spread * gain).astype(BF16).reshape(heads * rows, width)
    return packed, scale.reshape(heads * rows, 1)


class Mixer:
    def __init__(self, q, mean_square, gain, first_position):
        self.rows, self.width = q.shape
        self.many, self.wide = PACK * self.rows, PACK * HEAD
        self.packed, self.scale = spread_queries(q, mean_square, gain)
        self.first_position = first_position
        self.mixed = [None] * (self.width // self.wide)
        self.total = [None] * (self.width // self.wide)

    def absorb(self, columns, first_key):
        many, wide, rows = self.many, self.wide, self.rows
        for g in range(len(self.mixed)):
            these = slice(g * many, (g + 1) * many)
            keys = columns(g * wide, wide)
            tokens = keys.shape[0]
            scores = lax.dot_general(
                self.packed[these, g * wide:(g + 1) * wide], keys, NT, preferred_element_type=F32
            ) * self.scale[these]
            key_at = lax.broadcasted_iota(jnp.int32, (PACK, rows, tokens), 2).reshape(many, tokens)
            query_at = lax.broadcasted_iota(jnp.int32, (PACK, rows, tokens), 1).reshape(many, tokens)
            seen = key_at <= query_at + (self.first_position - first_key)
            weights = jnp.where(seen, jnp.exp2(scores), 0.0)
            total = sum(weights[:, i:i + 128] for i in range(0, tokens, 128))
            mixed = dot(weights.astype(BF16), columns(self.width + g * wide, wide))
            self.total[g] = total if self.total[g] is None else self.total[g] + total
            self.mixed[g] = mixed if self.mixed[g] is None else self.mixed[g] + mixed

    def result(self):
        outs = []
        for mixed, total in zip(self.mixed, self.total):
            mixed = mixed * (1.0 / jnp.sum(total, axis=-1, keepdims=True))
            mixed = mixed.reshape(PACK, self.rows, self.wide)
            row_head = lax.broadcasted_iota(jnp.int32, mixed.shape, 0)
            col_head = lax.broadcasted_iota(jnp.int32, mixed.shape, 2) // HEAD
            outs.append(jnp.sum(jnp.where(row_head == col_head, mixed, 0.0), axis=0).astype(BF16))
        return jnp.concatenate(outs, axis=-1)


def kernel(layers, seqs, x_hbm, wqkv_hbm, wo_hbm, gain_hbm, qk_hbm, out_ref,
           wq_all, wo_all, kv_all, kv_last, wkv, x_in, fine_in, cin, nxt, fine_out,
           guess_all, term_all, chain, gains_all, qk_raw, gain_raw, xs, ys,
           load, gather_send, gather_recv, spread_send, spread_recv,
           fine_send, fine_recv, guess_send, guess_recv, term_send, term_recv,
           cin_send, cin_recv, nxt_send, nxt_recv, hop_send, hop_recv, gain_send, gain_recv):
    layer = lax.axis_index("layer")
    seq = lax.axis_index("seq")
    units, unit, width = x_in.shape
    inner = width // 2
    group = layer // GROUP
    inside = lax.rem(layer, GROUP)
    member = inside // 2
    core = lax.rem(seq, 2)
    side = lax.rem(seq // 2, 2)
    even = lax.rem(layer, 2) == 0
    odd = jnp.logical_not(even)
    sibling = seq + 1 - 2 * core
    right, left = lax.rem(seq + 2, seqs), lax.rem(seq + seqs - 2, seqs)
    across = lax.rem(seq + 4, seqs)
    groups = layers // GROUP

    barrier = pltpu.get_barrier_semaphore()
    for other in (sibling, right, left):
        pl.semaphore_signal(barrier, inc=1, device_id={"seq": other}, device_id_type=MESH)
    leads = group == 0
    pair = jnp.logical_and(leads, jnp.logical_and(even, member >= 2))
    partner = 5 - member
    crossed = jnp.logical_and(group == 1, jnp.logical_and(even, member < 2))
    below = jnp.logical_and(even, group > 0)
    above = jnp.logical_and(even, group < groups - 1)

    def greet(when, other):
        @pl.when(when)
        def _():
            pl.semaphore_signal(barrier, inc=1, device_id={"layer": other}, device_id_type=MESH)

    for step in range(1, GROUP):
        other = group * GROUP + lax.rem(inside + step, GROUP)
        greet(jnp.logical_or(even, lax.rem(inside + step, 2) == 0), other)
    greet(below, layer - GROUP)
    greet(above, layer + GROUP)
    greet(pair, GROUP + 2 * (3 - member))
    greet(crossed, 2 * (3 - member))

    def count(when, amount):
        return jnp.where(when, amount, 0)

    greeted = (3 + jnp.where(even, GROUP - 1, MEMBERS) + count(below, 1) + count(above, 1) + count(crossed, 1)
               + count(pair, 1))

    loads = [
        pltpu.make_async_copy(x_hbm, x_in, load.at[0]),
        pltpu.make_async_copy(gain_hbm, gain_raw, load.at[1]),
        pltpu.make_async_copy(qk_hbm, qk_raw, load.at[2]),
        pltpu.make_async_copy(wqkv_hbm.at[1], wkv.at[0], load.at[3]),
        pltpu.make_async_copy(wqkv_hbm.at[2], wkv.at[1], load.at[4]),
        pltpu.make_async_copy(wqkv_hbm.at[0], wq_all.at[member], load.at[5]),
        pltpu.make_async_copy(wo_hbm, wo_all.at[member], load.at[6]),
    ]
    for copy in loads:
        copy.start()
    for copy in loads[:3]:
        copy.wait()
    gains_all[member, 0:1, :] = gain_raw[...]
    gains_all[member, 1:2, :] = jnp.concatenate([qk_raw[0:1, :]] * (inner // HEAD) + [qk_raw[1:2, :]] * (inner // HEAD), axis=-1)
    for copy in loads[3:]:
        copy.wait()
    norm_gain = gains_all[member, 0:1, :]
    query_gain = gains_all[member, 1:2, 0:inner]
    key_gain = gains_all[member, 1:2, inner:width]

    def remote(src, dst, send, recv, **target):
        return pltpu.make_async_remote_copy(
            src_ref=src, dst_ref=dst, send_sem=send, recv_sem=recv, device_id=target, device_id_type=MESH)

    def member_layer(m):
        return group * GROUP + 2 * m

    mine, others = 2 * side + core, 2 * (1 - side) + core

    def nth(step):
        return lax.rem(member + step + MEMBERS, MEMBERS)

    def part(m, quarter, p):
        if p in STATE_PARTS:
            p = p - STATE_PARTS[0]
            return kv_all.at[m, 2 * quarter + p // 2].at[pl.ds((p % 2) * (2 * unit), 2 * unit)]
        ref = (wq_all if p < 2 else wo_all).at[m, quarter]
        rows = ref.shape[0] // 2
        return ref.at[pl.ds((p % 2) * rows, rows)]

    def spread_copy(slot, m, quarter, p, **target):
        ref = part(m, quarter, p)
        return remote(ref, ref, spread_send.at[slot], spread_recv.at[m, quarter, p], **target)

    def hand(m, quarter, p, book=None, **target):
        book = sent if book is None else book
        spread_copy(len(book), m, quarter, p, **target).start()
        book.append(p)

    def await_part(m, quarter, p):
        spread_copy(0, m, quarter, p, seq=sibling).wait_recv()

    def spread_first(step, parts):
        for p in parts:
            hand(member, mine, p, layer=member_layer(nth(step)))

    def spread_on(moves):
        for kind, step, p in moves:
            m = nth(step)
            quarter = others if kind == "side" else mine
            await_part(m, quarter, p)
            if kind == "near" and (step == -1) == (p in ONWARD):
                hand(m, mine, p, layer=member_layer(nth(-step)))
            if kind != "side":
                hand(m, mine, p, seq=right if p % 2 == 0 else left)
            hand(m, quarter, p, seq=sibling)

    def spread_end(m):
        for p in WEIGHT_PARTS + STATE_PARTS:
            await_part(m, 2 * side + 1 - core, p)
            await_part(m, 2 * (1 - side) + 1 - core, p)

    def pair_first(parts):
        for p in parts:
            hand(member, mine, p, pair_sent, layer=member_layer(partner))

    def pair_near(parts):
        for p in parts:
            await_part(partner, mine, p)
            hand(partner, mine, p, pair_sent, seq=right if p % 2 == 0 else left)
            hand(partner, mine, p, pair_sent, seq=sibling)

    def pair_side(parts):
        for p in parts:
            await_part(partner, others, p)
            hand(partner, others, p, pair_sent, seq=sibling)

    def spread_drain(book):
        for slot, p in enumerate(book):
            spread_copy(slot, member, mine, p, seq=sibling).wait_send()

    later = jnp.logical_and(even, group > 0)
    sent, pair_sent = [], []

    def exact(source, ready, first, kv, send, recv, meet, pushed, gathered):
        copies = []
        order = [lax.rem(first + i, MEMBERS) if not isinstance(first, int) else i for i in UNIT_ORDER]

        def at(block, u):
            return kv(block).at[pl.ds(u * unit, unit)]

        def push(block, u, target):
            copy = remote(at(block, u), at(block, u), send.at[len(copies)], recv.at[block, u], seq=target)
            copy.start()
            copies.append(copy)

        def arrived(block, u):
            remote(at(block, u), at(block, u), send.at[0], recv.at[block, u], seq=sibling).wait_recv()

        same = lax.broadcasted_iota(jnp.int32, (inner, inner), 0) // HEAD
        same = (same == lax.broadcasted_iota(jnp.int32, (inner, inner), 1) // HEAD).astype(BF16)
        for k, u in enumerate(order):
            ready(u)
            here = pl.ds(u * unit, unit)
            x = source[u].astype(F32)
            xs[here, :] = x
            mean_square = jnp.mean(x * x, axis=-1, keepdims=True)
            y = (x * norm_gain).astype(BF16)
            ys[here, :] = y
            key = dot(y, wkv[0].reshape(width, inner))
            head_square = dot((key * key).astype(BF16), same) / HEAD
            key = key * lax.rsqrt(head_square + EPS * (mean_square + EPS)) * key_gain
            at(seq, u)[:, 0:inner] = key.astype(BF16)
            value = dot(y, wkv[1].reshape(width, inner)) * lax.rsqrt(mean_square + EPS)
            at(seq, u)[:, inner:width] = value.astype(BF16)
            if k == 0:
                meet()
            push(seq, u, right)
            push(seq, u, left)
            push(seq, u, sibling)
        pushed()
        x = xs[...]
        mean_square = jnp.mean(x * x, axis=-1, keepdims=True)
        q = dot(ys[...], wq_all[member].reshape(width, inner))
        mixer = Mixer(q, mean_square, query_gain, seq * units * unit)

        def absorb(block):
            chip = block // 2

            def columns(start, size):
                return kv(pl.ds(2 * chip, 2))[:, :, start:start + size].reshape(2 * units * unit, size)

            mixer.absorb(columns, chip * (2 * units * unit))

        for u in order:
            arrived(sibling, u)
        absorb(seq)
        for k, u in enumerate(order):
            arrived(left, u)
            if k % 2 == 0:
                push(left, u, right)
            push(left, u, sibling)
            arrived(right, u)
            if k % 2 == 1:
                push(right, u, left)
            push(right, u, sibling)
        for side_block, step in ((left, seqs - 2), (right, 2)):
            for u in order:
                arrived(lax.rem(sibling + step, seqs), u)
            absorb(side_block)
        for u in order:
            arrived(across, u)
            push(across, u, sibling)
        for u in order:
            arrived(lax.rem(sibling + 4, seqs), u)
        gathered()
        absorb(across)
        branch = dot(mixer.result(), wo_all[member].reshape(inner, width))
        return x, branch, copies

    def held(block):
        return kv_all.at[member, block]

    def last(block):
        return kv_last.at[block]

    def fine_copy(u, target):
        return remote(fine_out.at[u], fine_in.at[u], fine_send.at[u], fine_recv.at[u], layer=target)

    @pl.when(even)
    def _():
        for u in range(units):
            fine_in[u] = x_in[u]

    def fine_ready(u):
        @pl.when(odd)
        def _():
            if u == UNIT_ORDER[0]:
                pl.semaphore_wait(barrier, greeted)
            fine_copy(u, layer - 1).wait_recv()

    def meet():
        @pl.when(even)
        def _():
            pl.semaphore_wait(barrier, greeted)

    def pushed():
        @pl.when(later)
        def _():
            spread_first(1, WEIGHT_PARTS)
            spread_first(-1, WEIGHT_PARTS)
            for step in (1, 2, 3):
                gain_copy(step).start()

        @pl.when(pair)
        def _():
            pair_first(WEIGHT_PARTS)
            gain_to(partner, 0).start()

    def gathered():
        @pl.when(later)
        def _():
            spread_first(-1, (7, 4, 5, 6))
            spread_first(1, (4,))
            spread_on(EARLY)

    def nothing():
        pass

    def gain_to(m, slot):
        ref = gains_all.at[member]
        return remote(ref, ref, gain_send.at[slot], gain_recv.at[member], layer=member_layer(m))

    def gain_copy(step):
        return gain_to(nth(step), step - 1)

    x, branch, copies = exact(fine_in, fine_ready, 0, held, gather_send.at[0], gather_recv.at[0], meet, pushed, gathered)
    fine_out[...] = (x + branch).astype(BF16).reshape(units, unit, width)

    def pair_home(u):
        return 2 if u in (1, 2) else 3

    def home(u):
        first = jnp.where(inside < 4, 2, 2 * pair_home(u))
        return jnp.where(leads, first, group * GROUP + 2 * u)

    def guess_copy(u):
        ref = guess_all.at[member, u]
        return remote(ref, ref, guess_send.at[u], guess_recv.at[member, u], layer=home(u))

    def term_copy(u):
        return remote(fine_out.at[u], term_all.at[member, u], term_send.at[u], term_recv.at[member, u], layer=home(u))

    def start_copy(u):
        return remote(fine_out.at[u], chain.at[1, u], term_send.at[u], hop_recv.at[u], layer=layer + 1)

    def guess_goes(u):
        return jnp.logical_or(jnp.logical_and(later, u != member), jnp.logical_and(pair, pair_home(u) != member))

    @pl.when(odd)
    def _():
        @pl.when(layer == 1)
        def _():
            for u in FIRST_ORDER:
                start_copy(u).start()
            out_ref[...] = fine_out[...]

        @pl.when(layer > 1)
        def _():
            for u in range(units):
                term_copy(u).start()

        for copy in copies:
            copy.wait_send()
        for u in range(units):
            term_copy(u).wait_send()

        @pl.when(layer > 1)
        def _():
            for u in range(units):
                remote(chain.at[0, 0], nxt.at[u], nxt_send.at[0, 0], nxt_recv.at[u], layer=layer - 1).wait_recv()
            out_ref[...] = nxt[...]

    def cin_copy(m, u):
        return remote(chain.at[m, u], cin.at[u], cin_send.at[m, u], cin_recv.at[u], layer=member_layer(m))

    def nxt_copy(m, u):
        return remote(chain.at[m + 1, u], nxt.at[u], nxt_send.at[m, u], nxt_recv.at[u], layer=member_layer(m) + 1)

    def hop_copy(u, target):
        return remote(chain.at[MEMBERS, u], chain.at[0, u], hop_send.at[u], hop_recv.at[u], layer=target)

    def guess_wait(m, u):
        ref = guess_all.at[m, u]
        remote(ref, ref, guess_send.at[0], guess_recv.at[m, u], layer=layer + 1).wait_recv()

    def term_wait(m, u):
        ref = term_all.at[m, u]
        remote(ref, ref, term_send.at[0], term_recv.at[m, u], layer=layer + 1).wait_recv()

    def gain_wait(m):
        remote(gains_all.at[m], gains_all.at[m], gain_send.at[0], gain_recv.at[m], seq=sibling).wait_recv()

    def coarse_step(m, rows, correction, first_position):
        x = rows.astype(F32)
        mean_square = jnp.mean(x * x, axis=-1, keepdims=True)
        q = dot((x * gains_all[m, 0:1, :]).astype(BF16), wq_all[m].reshape(width, inner))

        def columns(start, size):
            return kv_all[m, :, :, start:start + size].reshape(seqs * units * unit, size)

        mixer = Mixer(q, mean_square, gains_all[m, 1:2, 0:inner], first_position)
        mixer.absorb(columns, 0)
        return (x + 2.0 * dot(mixer.result(), wo_all[m].reshape(inner, width)) + correction).astype(BF16)

    @pl.when(even)
    def _():
        for u in UNIT_ORDER:
            fine_copy(u, layer + 1).start()
        guess_all[member] = (x + 2.0 * branch).astype(BF16).reshape(units, unit, width)

    @pl.when(later)
    def _():
        spread_first(1, (5, 6, 7))

    @pl.when(pair)
    def _():
        pair_first(STATE_PARTS)
        pair_near((0, 1, 2))

    for u in range(units):
        @pl.when(guess_goes(u))
        def _():
            guess_copy(u).start()

    def hop_arrives(u):
        hop_copy(u, layer - 1).wait_recv()

    def lead_copy(u):
        return remote(chain.at[2, u], chain.at[2, u], hop_send.at[u], hop_recv.at[u], layer=2 * pair_home(u))

    def lead_nxt(u):
        return remote(chain.at[2, u], nxt.at[u], nxt_send.at[1, u], nxt_recv.at[u], layer=layer + 1)

    def step_one(m, u):
        term_wait(m, u)
        correction = term_all[m, u].astype(F32) - guess_all[m, u].astype(F32)
        chain[m + 1, u] = coarse_step(m, chain[m, u], correction, (seq * units + u) * unit)

    @pl.when(layer == 2)
    def _():
        for u in FIRST_ORDER:
            hop_arrives(u)
            step_one(1, u)
            lead_copy(u).start()
            lead_nxt(u).start()
        cin[...] = chain[1]

    def pair_units(body):
        for m in (2, 3):
            @pl.when(member == m)
            def _():
                for u in FIRST_ORDER:
                    if pair_home(u) == m:
                        body(m, u)

    @pl.when(pair)
    def _():
        pair_near((3,))
        pair_side((0, 1, 2))
        pair_near((4,))
        pair_side((3,))
        pair_near((5, 6))
        pair_side((4,))
        pair_near((7,))
        pair_side((5, 6, 7))
        spread_end(partner)
        gain_wait(partner)

        def walk(mine_m, u):
            hop_arrives(u)
            if mine_m == 2:
                cin[u] = chain[2, u]
            else:
                cin_copy(2, u).start()
                guess_wait(2, u)
            step_one(2, u)
            if mine_m == 3:
                cin[u] = chain[3, u]
            else:
                cin_copy(3, u).start()
                guess_wait(3, u)
            step_one(3, u)
            hop_copy(u, GROUP + 2 * u).start()
            nxt_copy(2, u).start()
            nxt_copy(3, u).start()

        pair_units(walk)

    @pl.when(later)
    def _():
        spread_on(LATE)
        for step in (-1, 1, 2):
            spread_end(nth(step))
        for step in (1, 2, 3):
            gain_wait(nth(step))
        hop_copy(member, layer - GROUP).wait_recv()

        def advance(m, carry):
            @pl.when(m != member)
            def _():
                cin_copy(m, member).start()
                guess_wait(m, member)

            @pl.when(m == member)
            def _():
                cin[member] = chain[m, member]

            term_wait(m, member)
            correction = term_all[m, member].astype(F32) - guess_all[m, member].astype(F32)
            chain[m + 1, member] = coarse_step(m, chain[m, member], correction, (seq * units + member) * unit)

            @pl.when(jnp.logical_and(m == MEMBERS - 1, group < groups - 1))
            def _():
                hop_copy(member, layer + GROUP).start()

            nxt_copy(m, member).start()
            return carry

        lax.fori_loop(0, MEMBERS, advance, 0)

    def cin_comes(u):
        in_pair = jnp.logical_or(u == 1, u == 2)
        from_other = jnp.logical_or(jnp.logical_and(in_pair, member == 3), jnp.logical_and(jnp.logical_not(in_pair), member == 2))
        return jnp.logical_or(jnp.logical_and(later, u != member), jnp.logical_and(pair, from_other))

    def cin_ready(u):
        @pl.when(cin_comes(u))
        def _():
            remote(chain.at[0, 0], cin.at[u], cin_send.at[0, 0], cin_recv.at[u], layer=layer + 1).wait_recv()

    @pl.when(layer == 0)
    def _():
        out_ref[...] = fine_out[...]

    @pl.when(jnp.logical_and(even, layer > 0))
    def _():
        x, branch, more = exact(cin, cin_ready, member, last, gather_send.at[1], gather_recv.at[1], nothing, nothing, nothing)
        out_ref[...] = (x + branch).astype(BF16).reshape(units, unit, width)
        for copy in more:
            copy.wait_send()

    @pl.when(even)
    def _():
        for u in range(units):
            fine_copy(u, layer + 1).wait_send()
        for copy in copies:
            copy.wait_send()

    for u in range(units):
        @pl.when(guess_goes(u))
        def _():
            guess_copy(u).wait_send()

    @pl.when(layer == 2)
    def _():
        for u in range(units):
            lead_copy(u).wait_send()
            lead_nxt(u).wait_send()

    @pl.when(pair)
    def _():
        spread_drain(pair_sent)
        gain_to(partner, 0).wait_send()

        def drained(mine_m, u):
            cin_copy(5 - mine_m, u).wait_send()
            hop_copy(u, GROUP + 2 * u).wait_send()
            nxt_copy(2, u).wait_send()
            nxt_copy(3, u).wait_send()

        pair_units(drained)

    @pl.when(later)
    def _():
        spread_drain(sent)
        for step in (1, 2, 3):
            gain_copy(step).wait_send()

        def drain(m, carry):
            nxt_copy(m, member).wait_send()

            @pl.when(m != member)
            def _():
                cin_copy(m, member).wait_send()

            return carry

        lax.fori_loop(0, MEMBERS, drain, 0)

        @pl.when(group < groups - 1)
        def _():
            hop_copy(member, layer + GROUP).wait_send()


def solution(mesh):
    layers, seqs = mesh.shape["layer"], mesh.shape["seq"]

    def on_device(states, w_qkv, w_out, norm_gain, qk_gain):
        rows, width = states.shape[1:]
        inner = w_out.shape[1]
        unit = rows // MEMBERS
        hbm = pl.BlockSpec(memory_space=pl.ANY)
        dma = pltpu.SemaphoreType.DMA
        state = pltpu.VMEM((MEMBERS, unit, width), BF16)
        rows_of = pltpu.VMEM((MEMBERS, MEMBERS, unit, width), BF16)
        out = pl.pallas_call(
            functools.partial(kernel, layers, seqs),
            out_shape=jax.ShapeDtypeStruct((MEMBERS, unit, width), BF16),
            in_specs=[hbm] * 5,
            out_specs=pl.BlockSpec(memory_space=pltpu.VMEM),
            scratch_shapes=[
                pltpu.VMEM((MEMBERS, QUARTERS, width // QUARTERS, inner), BF16),
                pltpu.VMEM((MEMBERS, QUARTERS, inner // QUARTERS, width), BF16),
                pltpu.VMEM((MEMBERS, seqs, rows, 2 * inner), BF16),
                pltpu.VMEM((seqs, rows, 2 * inner), BF16),
                pltpu.VMEM((2, QUARTERS, width // QUARTERS, inner), BF16),
                state, state, state, state, state, rows_of, rows_of,
                pltpu.VMEM((MEMBERS + 1, MEMBERS, unit, width), BF16),
                pltpu.VMEM((MEMBERS, 8, width), F32),
                pltpu.VMEM((2, HEAD), F32),
                pltpu.VMEM((1, width), F32),
                pltpu.VMEM((rows, width), F32),
                pltpu.VMEM((rows, width), BF16),
                dma((7,)), dma((2, 28)), dma((2, seqs, MEMBERS)), dma((96,)), dma((MEMBERS, QUARTERS, 8)),
                dma((4,)), dma((4,)), dma((4,)), dma((4, 4)), dma((4,)), dma((4, 4)),
                dma((4, 4)), dma((4,)), dma((4, 4)), dma((4,)), dma((4,)), dma((4,)), dma((3,)), dma((4,)),
            ],
            compiler_params=pltpu.CompilerParams(
                collective_id=0, has_side_effects=True, vmem_limit_bytes=56 << 20),
        )(
            states.reshape(MEMBERS, unit, width),
            w_qkv.reshape(3, QUARTERS, width // QUARTERS, inner),
            w_out.reshape(QUARTERS, inner // QUARTERS, width),
            norm_gain, qk_gain[0],
        )
        return out.reshape(1, rows, width)

    in_specs = (
        P("layer", "seq", None),
        P("layer", None, None, None),
        P("layer", None, None),
        P("layer", None),
        P("layer", None, None),
    )
    return jax.shard_map(
        on_device, mesh=mesh, in_specs=in_specs, out_specs=P("layer", "seq", None), check_vma=False
    )
```

```python
import functools

import jax
import jax.numpy as jnp
from jax import lax
from jax.experimental import pallas as pl
from jax.experimental.pallas import tpu as pltpu
from jax.sharding import PartitionSpec as P

EPS = 1e-06
MESH = pl.DeviceIdType.MESH
F32 = jnp.float32
BF16 = jnp.bfloat16
NT = (((1,), (1,)), ((), ()))
LOG2E = 1.4426950408889634
HEAD = 64
PACK = 4
MEMBERS = 4
GROUP = 2 * MEMBERS
QUARTERS = 4
WEIGHT_PARTS = (0, 1, 2, 3)
STATE_PARTS = (4, 5, 6, 7)
ONWARD = (4, 5, 6)

FIRST_ORDER = (0, 1, 3, 2)
UNIT_ORDER = (0, 1, 3, 2)
EARLY = (("near", -1, 0), ("near", 1, 0), ("near", -1, 1), ("near", 1, 1), ("near", -1, 2), ("near", 1, 2))
LATE = (
    ("near", -1, 3), ("near", 1, 3), ("side", -1, 0), ("side", -1, 1), ("near", -1, 4), ("near", 1, 7),
    ("side", 1, 0), ("side", 1, 1), ("near", 1, 4), ("side", -1, 2), ("side", -1, 3), ("near", 1, 5),
    ("side", 1, 2), ("side", 1, 3), ("near", -1, 5), ("near", 1, 6), ("side", -1, 4), ("side", 1, 7),
    ("near", -1, 6), ("far", 2, 0), ("side", 1, 4), ("side", 1, 5), ("near", -1, 7), ("far", 2, 1),
    ("side", -1, 5), ("side", 1, 6), ("far", 2, 2), ("far", 2, 4), ("side", -1, 6), ("side", -1, 7),
    ("far", 2, 3), ("far", 2, 5), ("side", 2, 0), ("side", 2, 1), ("far", 2, 7), ("far", 2, 6),
    ("side", 2, 2), ("side", 2, 3), ("side", 2, 4), ("side", 2, 5), ("side", 2, 6), ("side", 2, 7),
)


def dot(a, b):
    return jnp.dot(a, b, preferred_element_type=F32)


def spread_queries(q, mean_square, gain):
    rows, width = q.shape
    heads = width // HEAD
    row_head = lax.broadcasted_iota(jnp.int32, (heads, rows, width), 0)
    col_head = lax.broadcasted_iota(jnp.int32, (heads, rows, width), 2) // HEAD
    spread = jnp.where(row_head == col_head, q[None], 0.0)
    head_square = jnp.sum(spread * spread, axis=-1, keepdims=True) / HEAD
    scale = lax.rsqrt(head_square + EPS * (mean_square[None] + EPS)) * (LOG2E / 8.0)
    packed = (spread * gain).astype(BF16).reshape(heads * rows, width)
    return packed, scale.reshape(heads * rows, 1)


class Mixer:
    def __init__(self, q, mean_square, gain, first_position):
        self.rows, self.width = q.shape
        self.many, self.wide = PACK * self.rows, PACK * HEAD
        self.packed, self.scale = spread_queries(q, mean_square, gain)
        self.first_position = first_position
        self.mixed = [None] * (self.width // self.wide)
        self.total = [None] * (self.width // self.wide)

    def absorb(self, columns, first_key):
        many, wide, rows = self.many, self.wide, self.rows
        for g in range(len(self.mixed)):
            these = slice(g * many, (g + 1) * many)
            keys = columns(g * wide, wide)
            tokens = keys.shape[0]
            scores = lax.dot_general(
                self.packed[these, g * wide:(g + 1) * wide], keys, NT, preferred_element_type=F32
            ) * self.scale[these]
            key_at = lax.broadcasted_iota(jnp.int32, (PACK, rows, tokens), 2).reshape(many, tokens)
            query_at = lax.broadcasted_iota(jnp.int32, (PACK, rows, tokens), 1).reshape(many, tokens)
            seen = key_at <= query_at + (self.first_position - first_key)
            weights = jnp.where(seen, jnp.exp2(scores), 0.0)
            total = sum(weights[:, i:i + 128] for i in range(0, tokens, 128))
            mixed = dot(weights.astype(BF16), columns(self.width + g * wide, wide))
            self.total[g] = total if self.total[g] is None else self.total[g] + total
            self.mixed[g] = mixed if self.mixed[g] is None else self.mixed[g] + mixed

    def result(self):
        outs = []
        for mixed, total in zip(self.mixed, self.total):
            mixed = mixed * (1.0 / jnp.sum(total, axis=-1, keepdims=True))
            mixed = mixed.reshape(PACK, self.rows, self.wide)
            row_head = lax.broadcasted_iota(jnp.int32, mixed.shape, 0)
            col_head = lax.broadcasted_iota(jnp.int32, mixed.shape, 2) // HEAD
            outs.append(jnp.sum(jnp.where(row_head == col_head, mixed, 0.0), axis=0).astype(BF16))
        return jnp.concatenate(outs, axis=-1)


def kernel(layers, seqs, x_hbm, wqkv_hbm, wo_hbm, gain_hbm, qk_hbm, out_ref,
           wq_all, wo_all, kv_all, kv_last, wkv, x_in, fine_in, cin, nxt, fine_out,
           guess_all, term_all, chain, gains_all, qk_raw, gain_raw, xs, ys,
           load, gather_send, gather_recv, spread_send, spread_recv,
           fine_send, fine_recv, guess_send, guess_recv, term_send, term_recv,
           cin_send, cin_recv, nxt_send, nxt_recv, hop_send, hop_recv, gain_send, gain_recv):
    layer = lax.axis_index("layer")
    seq = lax.axis_index("seq")
    units, unit, width = x_in.shape
    inner = width // 2
    group = layer // GROUP
    inside = lax.rem(layer, GROUP)
    member = inside // 2
    core = lax.rem(seq, 2)
    side = lax.rem(seq // 2, 2)
    even = lax.rem(layer, 2) == 0
    odd = jnp.logical_not(even)
    sibling = seq + 1 - 2 * core
    right, left = lax.rem(seq + 2, seqs), lax.rem(seq + seqs - 2, seqs)
    across = lax.rem(seq + 4, seqs)
    groups = layers // GROUP

    barrier = pltpu.get_barrier_semaphore()
    for other in (sibling, right, left):
        pl.semaphore_signal(barrier, inc=1, device_id={"seq": other}, device_id_type=MESH)
    leads = group == 0
    pair = jnp.logical_and(leads, jnp.logical_and(even, member >= 2))
    partner = 5 - member
    crossed = jnp.logical_and(group == 1, jnp.logical_and(even, member < 2))
    below = jnp.logical_and(even, group > 0)
    above = jnp.logical_and(even, group < groups - 1)

    def greet(when, other):
        @pl.when(when)
        def _():
            pl.semaphore_signal(barrier, inc=1, device_id={"layer": other}, device_id_type=MESH)

    for step in range(1, GROUP):
        other = group * GROUP + lax.rem(inside + step, GROUP)
        greet(jnp.logical_or(even, lax.rem(inside + step, 2) == 0), other)
    greet(below, layer - GROUP)
    greet(above, layer + GROUP)
    greet(pair, GROUP + 2 * (3 - member))
    greet(crossed, 2 * (3 - member))

    def count(when, amount):
        return jnp.where(when, amount, 0)

    greeted = (3 + jnp.where(even, GROUP - 1, MEMBERS) + count(below, 1) + count(above, 1) + count(crossed, 1)
               + count(pair, 1))

    loads = [
        pltpu.make_async_copy(x_hbm, x_in, load.at[0]),
        pltpu.make_async_copy(gain_hbm, gain_raw, load.at[1]),
        pltpu.make_async_copy(qk_hbm, qk_raw, load.at[2]),
        pltpu.make_async_copy(wqkv_hbm.at[1], wkv.at[0], load.at[3]),
        pltpu.make_async_copy(wqkv_hbm.at[2], wkv.at[1], load.at[4]),
        pltpu.make_async_copy(wqkv_hbm.at[0], wq_all.at[member], load.at[5]),
        pltpu.make_async_copy(wo_hbm, wo_all.at[member], load.at[6]),
    ]
    for copy in loads:
        copy.start()
    for copy in loads[:3]:
        copy.wait()
    gains_all[member, 0:1, :] = gain_raw[...]
    gains_all[member, 1:2, :] = jnp.concatenate([qk_raw[0:1, :]] * (inner // HEAD) + [qk_raw[1:2, :]] * (inner // HEAD), axis=-1)
    for copy in loads[3:]:
        copy.wait()
    norm_gain = gains_all[member, 0:1, :]
    query_gain = gains_all[member, 1:2, 0:inner]
    key_gain = gains_all[member, 1:2, inner:width]

    def remote(src, dst, send, recv, **target):
        return pltpu.make_async_remote_copy(
            src_ref=src, dst_ref=dst, send_sem=send, recv_sem=recv, device_id=target, device_id_type=MESH)

    def member_layer(m):
        return group * GROUP + 2 * m

    mine, others = 2 * side + core, 2 * (1 - side) + core

    def nth(step):
        return lax.rem(member + step + MEMBERS, MEMBERS)

    def part(m, quarter, p):
        if p in STATE_PARTS:
            p = p - STATE_PARTS[0]
            return kv_all.at[m, 2 * quarter + p // 2].at[pl.ds((p % 2) * (2 * unit), 2 * unit)]
        ref = (wq_all if p < 2 else wo_all).at[m, quarter]
        rows = ref.shape[0] // 2
        return ref.at[pl.ds((p % 2) * rows, rows)]

    def spread_copy(slot, m, quarter, p, **target):
        ref = part(m, quarter, p)
        return remote(ref, ref, spread_send.at[slot], spread_recv.at[m, quarter, p], **target)

    def hand(m, quarter, p, book=None, **target):
        book = sent if book is None else book
        spread_copy(len(book), m, quarter, p, **target).start()
        book.append(p)

    def await_part(m, quarter, p):
        spread_copy(0, m, quarter, p, seq=sibling).wait_recv()

    def spread_first(step, parts):
        for p in parts:
            hand(member, mine, p, layer=member_layer(nth(step)))

    def spread_on(moves):
        for kind, step, p in moves:
            m = nth(step)
            quarter = others if kind == "side" else mine
            await_part(m, quarter, p)
            if kind == "near" and (step == -1) == (p in ONWARD):
                hand(m, mine, p, layer=member_layer(nth(-step)))
            if kind != "side":
                hand(m, mine, p, seq=right if p % 2 == 0 else left)
            hand(m, quarter, p, seq=sibling)

    def spread_end(m):
        for p in WEIGHT_PARTS + STATE_PARTS:
            await_part(m, 2 * side + 1 - core, p)
            await_part(m, 2 * (1 - side) + 1 - core, p)

    def pair_first(parts):
        for p in parts:
            hand(member, mine, p, pair_sent, layer=member_layer(partner))

    def pair_near(parts):
        for p in parts:
            await_part(partner, mine, p)
            hand(partner, mine, p, pair_sent, seq=right if p % 2 == 0 else left)
            hand(partner, mine, p, pair_sent, seq=sibling)

    def pair_side(parts):
        for p in parts:
            await_part(partner, others, p)
            hand(partner, others, p, pair_sent, seq=sibling)

    def spread_drain(book):
        for slot, p in enumerate(book):
            spread_copy(slot, member, mine, p, seq=sibling).wait_send()

    later = jnp.logical_and(even, group > 0)
    sent, pair_sent = [], []

    def exact(source, ready, first, kv, send, recv, meet, pushed, gathered):
        copies = []
        order = [lax.rem(first + i, MEMBERS) if not isinstance(first, int) else i for i in UNIT_ORDER]

        def at(block, u):
            return kv(block).at[pl.ds(u * unit, unit)]

        def push(block, u, target):
            copy = remote(at(block, u), at(block, u), send.at[len(copies)], recv.at[block, u], seq=target)
            copy.start()
            copies.append(copy)

        def arrived(block, u):
            remote(at(block, u), at(block, u), send.at[0], recv.at[block, u], seq=sibling).wait_recv()

        same = lax.broadcasted_iota(jnp.int32, (inner, inner), 0) // HEAD
        same = (same == lax.broadcasted_iota(jnp.int32, (inner, inner), 1) // HEAD).astype(BF16)
        for k, u in enumerate(order):
            ready(u)
            here = pl.ds(u * unit, unit)
            x = source[u].astype(F32)
            xs[here, :] = x
            mean_square = jnp.mean(x * x, axis=-1, keepdims=True)
            y = (x * norm_gain).astype(BF16)
            ys[here, :] = y
            key = dot(y, wkv[0].reshape(width, inner))
            head_square = dot((key * key).astype(BF16), same) / HEAD
            key = key * lax.rsqrt(head_square + EPS * (mean_square + EPS)) * key_gain
            at(seq, u)[:, 0:inner] = key.astype(BF16)
            value = dot(y, wkv[1].reshape(width, inner)) * lax.rsqrt(mean_square + EPS)
            at(seq, u)[:, inner:width] = value.astype(BF16)
            if k == 0:
                meet()
            push(seq, u, right)
            push(seq, u, left)
            push(seq, u, sibling)
        pushed()
        x = xs[...]
        mean_square = jnp.mean(x * x, axis=-1, keepdims=True)
        q = dot(ys[...], wq_all[member].reshape(width, inner))
        mixer = Mixer(q, mean_square, query_gain, seq * units * unit)

        def absorb(block):
            chip = block // 2

            def columns(start, size):
                return kv(pl.ds(2 * chip, 2))[:, :, start:start + size].reshape(2 * units * unit, size)

            mixer.absorb(columns, chip * (2 * units * unit))

        for u in order:
            arrived(sibling, u)
        absorb(seq)
        for k, u in enumerate(order):
            arrived(left, u)
            if k % 2 == 0:
                push(left, u, right)
            push(left, u, sibling)
            arrived(right, u)
            if k % 2 == 1:
                push(right, u, left)
            push(right, u, sibling)
        for side_block, step in ((left, seqs - 2), (right, 2)):
            for u in order:
                arrived(lax.rem(sibling + step, seqs), u)
            absorb(side_block)
        for u in order:
            arrived(across, u)
            push(across, u, sibling)
        for u in order:
            arrived(lax.rem(sibling + 4, seqs), u)
        gathered()
        absorb(across)
        branch = dot(mixer.result(), wo_all[member].reshape(inner, width))
        return x, branch, copies

    def held(block):
        return kv_all.at[member, block]

    def last(block):
        return kv_last.at[block]

    def fine_copy(u, target):
        return remote(fine_out.at[u], fine_in.at[u], fine_send.at[u], fine_recv.at[u], layer=target)

    @pl.when(even)
    def _():
        for u in range(units):
            fine_in[u] = x_in[u]

    def fine_ready(u):
        @pl.when(odd)
        def _():
            if u == UNIT_ORDER[0]:
                pl.semaphore_wait(barrier, greeted)
            fine_copy(u, layer - 1).wait_recv()

    def meet():
        @pl.when(even)
        def _():
            pl.semaphore_wait(barrier, greeted)

    def pushed():
        @pl.when(later)
        def _():
            spread_first(1, WEIGHT_PARTS)
            spread_first(-1, WEIGHT_PARTS)
            for step in (1, 2, 3):
                gain_copy(step).start()

        @pl.when(pair)
        def _():
            pair_first(WEIGHT_PARTS)
            gain_to(partner, 0).start()

    def gathered():
        @pl.when(later)
        def _():
            spread_first(-1, (7, 4, 5, 6))
            spread_first(1, (4,))
            spread_on(EARLY)

    def nothing():
        pass

    def gain_to(m, slot):
        ref = gains_all.at[member]
        return remote(ref, ref, gain_send.at[slot], gain_recv.at[member], layer=member_layer(m))

    def gain_copy(step):
        return gain_to(nth(step), step - 1)

    x, branch, copies = exact(fine_in, fine_ready, 0, held, gather_send.at[0], gather_recv.at[0], meet, pushed, gathered)
    fine_out[...] = (x + branch).astype(BF16).reshape(units, unit, width)

    def pair_home(u):
        return 2 if u in (1, 2) else 3

    def home(u):
        first = jnp.where(inside < 4, 2, 2 * pair_home(u))
        return jnp.where(leads, first, group * GROUP + 2 * u)

    def guess_copy(u):
        ref = guess_all.at[member, u]
        return remote(ref, ref, guess_send.at[u], guess_recv.at[member, u], layer=home(u))

    def term_copy(u):
        return remote(fine_out.at[u], term_all.at[member, u], term_send.at[u], term_recv.at[member, u], layer=home(u))

    def start_copy(u):
        return remote(fine_out.at[u], chain.at[1, u], term_send.at[u], hop_recv.at[u], layer=layer + 1)

    def guess_goes(u):
        return jnp.logical_or(jnp.logical_and(later, u != member), jnp.logical_and(pair, pair_home(u) != member))

    @pl.when(odd)
    def _():
        @pl.when(layer == 1)
        def _():
            for u in FIRST_ORDER:
                start_copy(u).start()
            out_ref[...] = fine_out[...]

        @pl.when(layer > 1)
        def _():
            for u in FIRST_ORDER:
                term_copy(u).start()

        for copy in copies:
            copy.wait_send()
        for u in range(units):
            term_copy(u).wait_send()

        @pl.when(layer > 1)
        def _():
            for u in range(units):
                remote(chain.at[0, 0], nxt.at[u], nxt_send.at[0, 0], nxt_recv.at[u], layer=layer - 1).wait_recv()
            out_ref[...] = nxt[...]

    def cin_copy(m, u):
        return remote(chain.at[m, u], cin.at[u], cin_send.at[m, u], cin_recv.at[u], layer=member_layer(m))

    def nxt_copy(m, u):
        return remote(chain.at[m + 1, u], nxt.at[u], nxt_send.at[m, u], nxt_recv.at[u], layer=member_layer(m) + 1)

    def hop_copy(u, target):
        return remote(chain.at[MEMBERS, u], chain.at[0, u], hop_send.at[u], hop_recv.at[u], layer=target)

    def guess_wait(m, u):
        ref = guess_all.at[m, u]
        remote(ref, ref, guess_send.at[0], guess_recv.at[m, u], layer=layer + 1).wait_recv()

    def term_wait(m, u):
        ref = term_all.at[m, u]
        remote(ref, ref, term_send.at[0], term_recv.at[m, u], layer=layer + 1).wait_recv()

    def gain_wait(m):
        remote(gains_all.at[m], gains_all.at[m], gain_send.at[0], gain_recv.at[m], seq=sibling).wait_recv()

    def coarse_step(m, rows, correction, first_position):
        x = rows.astype(F32)
        mean_square = jnp.mean(x * x, axis=-1, keepdims=True)
        q = dot((x * gains_all[m, 0:1, :]).astype(BF16), wq_all[m].reshape(width, inner))

        def columns(start, size):
            return kv_all[m, :, :, start:start + size].reshape(seqs * units * unit, size)

        mixer = Mixer(q, mean_square, gains_all[m, 1:2, 0:inner], first_position)
        mixer.absorb(columns, 0)
        return (x + 2.0 * dot(mixer.result(), wo_all[m].reshape(inner, width)) + correction).astype(BF16)

    @pl.when(even)
    def _():
        for u in UNIT_ORDER:
            fine_copy(u, layer + 1).start()
        guess_all[member] = (x + 2.0 * branch).astype(BF16).reshape(units, unit, width)

    @pl.when(later)
    def _():
        spread_first(1, (5, 6, 7))

    @pl.when(pair)
    def _():
        pair_first(STATE_PARTS)
        pair_near((0, 1, 2))

    for u in range(units):
        @pl.when(guess_goes(u))
        def _():
            guess_copy(u).start()

    def hop_arrives(u):
        hop_copy(u, layer - 1).wait_recv()

    def lead_copy(u):
        return remote(chain.at[2, u], chain.at[2, u], hop_send.at[u], hop_recv.at[u], layer=2 * pair_home(u))

    def lead_nxt(u):
        return remote(chain.at[2, u], nxt.at[u], nxt_send.at[1, u], nxt_recv.at[u], layer=layer + 1)

    def step_one(m, u):
        term_wait(m, u)
        correction = term_all[m, u].astype(F32) - guess_all[m, u].astype(F32)
        chain[m + 1, u] = coarse_step(m, chain[m, u], correction, (seq * units + u) * unit)

    @pl.when(layer == 2)
    def _():
        for u in FIRST_ORDER:
            hop_arrives(u)
            step_one(1, u)
            lead_copy(u).start()
            lead_nxt(u).start()
        cin[...] = chain[1]

    def pair_units(body):
        for m in (2, 3):
            @pl.when(member == m)
            def _():
                for u in FIRST_ORDER:
                    if pair_home(u) == m:
                        body(m, u)

    @pl.when(pair)
    def _():
        pair_near((3,))
        pair_side((0, 1, 2))
        pair_near((4,))
        pair_side((3,))
        pair_near((5, 6))
        pair_side((4,))
        pair_near((7,))
        pair_side((5, 6, 7))
        spread_end(partner)
        gain_wait(partner)

        def walk(mine_m, u):
            hop_arrives(u)
            if mine_m == 2:
                cin[u] = chain[2, u]
            else:
                cin_copy(2, u).start()
                guess_wait(2, u)
            step_one(2, u)
            if mine_m == 3:
                cin[u] = chain[3, u]
            else:
                cin_copy(3, u).start()
                guess_wait(3, u)
            step_one(3, u)
            hop_copy(u, GROUP + 2 * u).start()
            nxt_copy(2, u).start()
            nxt_copy(3, u).start()

        pair_units(walk)

    @pl.when(later)
    def _():
        spread_on(LATE)
        for step in (-1, 1, 2):
            spread_end(nth(step))
        for step in (1, 2, 3):
            gain_wait(nth(step))
        hop_copy(member, layer - GROUP).wait_recv()

        def advance(m, carry):
            @pl.when(m != member)
            def _():
                cin_copy(m, member).start()
                guess_wait(m, member)

            @pl.when(m == member)
            def _():
                cin[member] = chain[m, member]

            term_wait(m, member)
            correction = term_all[m, member].astype(F32) - guess_all[m, member].astype(F32)
            chain[m + 1, member] = coarse_step(m, chain[m, member], correction, (seq * units + member) * unit)

            @pl.when(jnp.logical_and(m == MEMBERS - 1, group < groups - 1))
            def _():
                hop_copy(member, layer + GROUP).start()

            nxt_copy(m, member).start()
            return carry

        lax.fori_loop(0, MEMBERS, advance, 0)

    def cin_comes(u):
        in_pair = jnp.logical_or(u == 1, u == 2)
        from_other = jnp.logical_or(jnp.logical_and(in_pair, member == 3), jnp.logical_and(jnp.logical_not(in_pair), member == 2))
        return jnp.logical_or(jnp.logical_and(later, u != member), jnp.logical_and(pair, from_other))

    def cin_ready(u):
        @pl.when(cin_comes(u))
        def _():
            remote(chain.at[0, 0], cin.at[u], cin_send.at[0, 0], cin_recv.at[u], layer=layer + 1).wait_recv()

    @pl.when(layer == 0)
    def _():
        out_ref[...] = fine_out[...]

    @pl.when(jnp.logical_and(even, layer > 0))
    def _():
        x, branch, more = exact(cin, cin_ready, member, last, gather_send.at[1], gather_recv.at[1], nothing, nothing, nothing)
        out_ref[...] = (x + branch).astype(BF16).reshape(units, unit, width)
        for copy in more:
            copy.wait_send()

    @pl.when(even)
    def _():
        for u in range(units):
            fine_copy(u, layer + 1).wait_send()
        for copy in copies:
            copy.wait_send()

    for u in range(units):
        @pl.when(guess_goes(u))
        def _():
            guess_copy(u).wait_send()

    @pl.when(layer == 2)
    def _():
        for u in range(units):
            lead_copy(u).wait_send()
            lead_nxt(u).wait_send()

    @pl.when(pair)
    def _():
        spread_drain(pair_sent)
        gain_to(partner, 0).wait_send()

        def drained(mine_m, u):
            cin_copy(5 - mine_m, u).wait_send()
            hop_copy(u, GROUP + 2 * u).wait_send()
            nxt_copy(2, u).wait_send()
            nxt_copy(3, u).wait_send()

        pair_units(drained)

    @pl.when(later)
    def _():
        spread_drain(sent)
        for step in (1, 2, 3):
            gain_copy(step).wait_send()

        def drain(m, carry):
            nxt_copy(m, member).wait_send()

            @pl.when(m != member)
            def _():
                cin_copy(m, member).wait_send()

            return carry

        lax.fori_loop(0, MEMBERS, drain, 0)

        @pl.when(group < groups - 1)
        def _():
            hop_copy(member, layer + GROUP).wait_send()


def solution(mesh):
    layers, seqs = mesh.shape["layer"], mesh.shape["seq"]

    def on_device(states, w_qkv, w_out, norm_gain, qk_gain):
        rows, width = states.shape[1:]
        inner = w_out.shape[1]
        unit = rows // MEMBERS
        hbm = pl.BlockSpec(memory_space=pl.ANY)
        dma = pltpu.SemaphoreType.DMA
        state = pltpu.VMEM((MEMBERS, unit, width), BF16)
        rows_of = pltpu.VMEM((MEMBERS, MEMBERS, unit, width), BF16)
        out = pl.pallas_call(
            functools.partial(kernel, layers, seqs),
            out_shape=jax.ShapeDtypeStruct((MEMBERS, unit, width), BF16),
            in_specs=[hbm] * 5,
            out_specs=pl.BlockSpec(memory_space=pltpu.VMEM),
            scratch_shapes=[
                pltpu.VMEM((MEMBERS, QUARTERS, width // QUARTERS, inner), BF16),
                pltpu.VMEM((MEMBERS, QUARTERS, inner // QUARTERS, width), BF16),
                pltpu.VMEM((MEMBERS, seqs, rows, 2 * inner), BF16),
                pltpu.VMEM((seqs, rows, 2 * inner), BF16),
                pltpu.VMEM((2, QUARTERS, width // QUARTERS, inner), BF16),
                state, state, state, state, state, rows_of, rows_of,
                pltpu.VMEM((MEMBERS + 1, MEMBERS, unit, width), BF16),
                pltpu.VMEM((MEMBERS, 8, width), F32),
                pltpu.VMEM((2, HEAD), F32),
                pltpu.VMEM((1, width), F32),
                pltpu.VMEM((rows, width), F32),
                pltpu.VMEM((rows, width), BF16),
                dma((7,)), dma((2, 28)), dma((2, seqs, MEMBERS)), dma((96,)), dma((MEMBERS, QUARTERS, 8)),
                dma((4,)), dma((4,)), dma((4,)), dma((4, 4)), dma((4,)), dma((4, 4)),
                dma((4, 4)), dma((4,)), dma((4, 4)), dma((4,)), dma((4,)), dma((4,)), dma((3,)), dma((4,)),
            ],
            compiler_params=pltpu.CompilerParams(
                collective_id=0, has_side_effects=True, vmem_limit_bytes=56 << 20),
        )(
            states.reshape(MEMBERS, unit, width),
            w_qkv.reshape(3, QUARTERS, width // QUARTERS, inner),
            w_out.reshape(QUARTERS, inner // QUARTERS, width),
            norm_gain, qk_gain[0],
        )
        return out.reshape(1, rows, width)

    in_specs = (
        P("layer", "seq", None),
        P("layer", None, None, None),
        P("layer", None, None),
        P("layer", None),
        P("layer", None, None),
    )
    return jax.shard_map(
        on_device, mesh=mesh, in_specs=in_specs, out_specs=P("layer", "seq", None), check_vma=False
    )
```
